256 devices in a mesh: cache: 32 (over y, z), head: 8 (over x, core).
Axes of the slice: x: 4, y: 4, z: 8, core: 2. Of those that a mesh axis runs over, the one named last changes fastest.
Arguments:
- candidates: bfloat16 [65536, 1024], P(('cache', 'head')), may hold values from -6 to 6
- proj_in: bfloat16 [2, 1024, 4096], P(None, None, 'head'), may hold values from -0.1875 to 0.1875
- proj_out: bfloat16 [2, 1024, 1024], P(None, 'head'), may hold values from -0.1875 to 0.1875
- page_pool: bfloat16 [32, 32, 2, 2, 128, 2048], P('cache', None, None, None, None, 'head'), may hold values from -6 to 6
- page_owner: int32 [64, 16, 1], P('cache'), may hold values from 0 to 31; in each aligned block of 32 rows (0 to 31, 32 to 63, ..., all dimensions but the last counted through in order) at most 2 rows name the same one
- history_pages: int32 [64], P('cache'), may hold values from 9 to 16, as said below
Outputs:
- scored: bfloat16 [65536, 1024], P(('cache', 'head'))
The draws below stay inside these ranges and needn't reach their ends.
Inputs may be any that keep to these rules, and one draw needn't show every extreme that they name: `page_owner`: in the pages of the users of one scoring group no owner is named more than 2 times, a bound that some block reaches. `history_pages`: some user has all 16 pages live.
All inputs are finite; a program needn't handle non-finite values.
Results may differ from the reference program's by a relative error of at most 0.02.
Values may be sent and summed in bfloat16 or wider, within the bound.
A program may use at most 128 MiB of HBM per device.

```python
import math
import jax
import jax.numpy as jnp
import numpy as np
from jax import lax

HEADS = 8
DH = 128
D = 1024
LAYERS = 2
USERS_DEV = 2
CAND = 1024
PAGE = 128
PAGES_USER = 16
CAP = 2
USERS = 64
ROWS = 65536
N_CACHE = 32
N_HEAD = 8


def draw_history_pages(key, part):
    key = jax.random.fold_in(key, 11)
    first_key, second_key = jax.random.split(key)
    lengths = jax.random.randint(first_key, (USERS,), PAGES_USER // 2 + 1, PAGES_USER + 1)
    chosen = jax.random.randint(second_key, (), 0, USERS)
    lengths = jnp.where(jnp.arange(USERS) == chosen, PAGES_USER, lengths)
    return lengths.astype(jnp.int32)


def steps_of(key, shape, pieces, smallest, top_value):
    loudness = 1.0
    for dim, blocks in pieces:
        draws = jax.random.uniform(jax.random.fold_in(jax.random.fold_in(key, 6), dim), (blocks,), jnp.float32, smallest / len(pieces), top_value / len(pieces))
        loudness = loudness * jnp.repeat(jnp.exp(draws), shape[dim] // blocks).reshape((-1,) + (1,) * (len(shape) - 1 - dim))
    return loudness


def assign_block(own_key, own, number, rows, count, top, limit, skew):
    order = jax.random.permutation(own_key, count)
    heavy_load, common = shares(count, rows * top, limit, skew, True), shares(count, rows * top, limit, skew, False)
    places = jnp.arange(count)

    def named(tallies, turn):
        used = int((tallies > 0).sum())
        fixed = max(1, used // 4)
        passed = fixed + (places - fixed + turn * (used - fixed)) % max(1, count - fixed)
        return jnp.zeros((count,), jnp.int32).at[order[jnp.where(places < fixed, places, passed)]].set(jnp.asarray(tallies, jnp.int32))

    tallies = jnp.where(number % 4 == 0, named(heavy_load, number // 4), named(common, number - number // 4 - 1))
    mixed = jax.random.permutation(jax.random.fold_in(own, 3), count)
    donor, sink = mixed[0:count // 2 * 2:2], mixed[1:count // 2 * 2:2]
    slack = jnp.minimum(tallies[donor] - 1, limit - tallies[sink]) // 2
    slack = jnp.where((donor == order[0]) | (sink == order[0]) | (tallies[sink] == 0), 0, jnp.maximum(slack, 0))
    passed = jax.random.randint(jax.random.fold_in(own, 4), (count // 2,), 0, 1 << 20) % (slack + 1)
    tallies = tallies.at[donor].add(-passed).at[sink].add(passed)
    members = jnp.searchsorted(jnp.cumsum(tallies), jnp.arange(rows * top), side="right").astype(jnp.int32)
    listing = members.reshape(top, rows).T
    listing = listing[jax.random.permutation(jax.random.fold_in(own, 1), rows)]
    turn = jax.random.randint(jax.random.fold_in(own, 2), (rows, 1), 0, top)
    return jnp.take_along_axis(listing, (jnp.arange(top)[None, :] + turn) % top, axis=1)


def shares(count, total, bound, slope, full):
    weights = [(1 << 20) // math.isqrt(grade ** slope) + 1 for grade in range(1, count + 1)]
    largest = bound if full else min(bound, max(-(-total // count), total * weights[0] // sum(weights)))
    least = 1 if total - largest >= count - 1 else 0
    counts, surplus = [largest] + [least] * (count - 1), total - largest - least * (count - 1)
    while surplus > 0:
        free = [i for i in range(1, count) if counts[i] < largest] or [i for i in range(1, count) if counts[i] < bound]
        pool, left = sum([weights[i] for i in free]), surplus
        for i in free:
            extra = min(bound - counts[i], max(1, left * weights[i] // pool), surplus)
            counts[i] = counts[i] + extra
            surplus = surplus - extra
    return np.array(counts)


def normal_values(stream_key, dims, scale, bound, pieces=(), kind=jnp.bfloat16):
    gain = steps_of(stream_key, dims, pieces, -0.22, 0.18) if pieces else 1.0
    array = jax.random.normal(stream_key, dims, jnp.float32) * scale * gain
    return jnp.minimum(jnp.maximum(array, -bound), bound).astype(kind)


def setup_inputs(seed: int = 0) -> dict:
    key_list = jax.random.split(jax.random.key(seed), 7)
    candidates = normal_values(key_list[0], (ROWS, D), 1.0, 6.0, ((0, 256),))
    proj_in = normal_values(key_list[1], (LAYERS, D, 4 * D), D ** -0.5, 0.1875, ((2, 8),))
    proj_out = normal_values(key_list[2], (LAYERS, D, D), D ** -0.5, 0.1875, ((1, 8),))
    page_pool = normal_values(key_list[3], (N_CACHE, N_CACHE, CAP, LAYERS, PAGE, 2 * D), 1.0, 6.0, ((0, 32), (5, 8)))
    page_owner_keys = jax.random.split(jax.random.fold_in(key_list[4], 1), USERS * PAGES_USER // (USERS_DEV * PAGES_USER))
    page_owner_turns = jax.random.permutation(jax.random.fold_in(key_list[4], 3), USERS * PAGES_USER // (USERS_DEV * PAGES_USER))
    page_owner = jax.vmap(lambda own, number: assign_block(jax.random.fold_in(key_list[4], 2), own, number, USERS_DEV * PAGES_USER, N_CACHE, 1, CAP, 2))(page_owner_keys, page_owner_turns).reshape((USERS, PAGES_USER, 1))
    history_pages = draw_history_pages(jax.random.fold_in(key_list[6], 71), 0)
    return dict(candidates=candidates, proj_in=proj_in, proj_out=proj_out, page_pool=page_pool, page_owner=page_owner, history_pages=history_pages)


def one_layer(state, history, w_in, w_out, lengths):
    group_rows = state.shape[0]
    xf = state.astype(jnp.float32)
    normed = (xf * lax.rsqrt(lax.optimization_barrier(jnp.mean(xf * xf, axis=-1, keepdims=True)) + 1e-06)).astype(jnp.bfloat16)
    act = jax.nn.silu(jnp.dot(normed, w_in, preferred_element_type=jnp.float32)).astype(jnp.bfloat16)
    act = act.reshape(USERS_DEV, CAND, HEADS, 4, DH)
    gate = act[:, :, :, 0, :]
    value = act[:, :, :, 1, :]
    query = act[:, :, :, 2, :]
    key = act[:, :, :, 3, :]
    hist = history.reshape(USERS_DEV, PAGES_USER * PAGE, HEADS, 2, DH)
    hist_key = hist[:, :, :, 0, :]
    hist_value = hist[:, :, :, 1, :]
    scale = DH ** (-0.5)
    live = jnp.arange(PAGES_USER * PAGE)[None, :] < (lengths * PAGE)[:, None]
    denom = (lengths * PAGE + 1).astype(jnp.float32)
    scores = jnp.einsum('uchd,uehd->uhce', query.astype(jnp.float32), hist_key.astype(jnp.float32)) * scale
    weights = jnp.where(live[:, None, None, :], jax.nn.silu(scores), 0.0) / denom[:, None, None, None]
    weights = weights.astype(jnp.bfloat16)
    own = lax.optimization_barrier(jnp.sum(query.astype(jnp.float32) * key.astype(jnp.float32), axis=-1)) * scale
    own_weight = (jax.nn.silu(own) / denom[:, None, None]).astype(jnp.bfloat16)
    attended = jnp.einsum('uhce,uehd->uchd', weights.astype(jnp.float32), hist_value.astype(jnp.float32))
    attended = attended + own_weight.astype(jnp.float32)[..., None] * value.astype(jnp.float32)
    attended = attended.reshape(group_rows, D)
    first = lax.optimization_barrier(jnp.mean(attended, axis=-1, keepdims=True))
    second = lax.optimization_barrier(jnp.mean(attended * attended, axis=-1, keepdims=True))
    gated = ((attended - first) * lax.rsqrt(second - first * first + 1e-05) * gate.reshape(group_rows, D).astype(jnp.float32)).astype(jnp.bfloat16)
    part_width = D // N_HEAD
    gated_parts = gated.reshape(group_rows, N_HEAD, part_width).astype(jnp.float32)
    out_parts = w_out.reshape(N_HEAD, part_width, D).astype(jnp.float32)
    partials = jnp.einsum('gnk,nke->nge', gated_parts, out_parts).astype(jnp.bfloat16)
    update = lax.optimization_barrier(jnp.sum(partials.astype(jnp.float32), axis=0))
    return (xf + update).astype(jnp.bfloat16)

def reference(candidates, proj_in, proj_out, page_pool, page_owner, history_pages):
    group_rows = USERS_DEV * CAND
    page_count = USERS_DEV * PAGES_USER

    def one_group(group):
        state = lax.dynamic_slice_in_dim(candidates, group * group_rows, group_rows, 0)
        owners = lax.dynamic_slice_in_dim(page_owner, group * USERS_DEV, USERS_DEV, 0)[:, :, 0].reshape(page_count)
        lengths = lax.dynamic_slice_in_dim(history_pages, group * USERS_DEV, USERS_DEV, 0)
        order = jnp.arange(page_count)
        earlier = (owners[:, None] == owners[None, :]) & (order[None, :] < order[:, None])
        slots = lax.optimization_barrier(jnp.sum(earlier.astype(jnp.int32), axis=1)).astype(jnp.int32)
        source_rows = (owners * CAP + slots).astype(jnp.int32)
        pool_group = lax.dynamic_index_in_dim(page_pool, group, 1, keepdims=False)
        pool_group = pool_group.reshape(N_CACHE * CAP, LAYERS, PAGE, 2 * D)
        picked = pool_group[source_rows]
        for layer in range(LAYERS):
            state = one_layer(state, picked[:, layer], proj_in[layer], proj_out[layer], lengths)
        return state
    result = lax.map(one_group, jnp.arange(N_CACHE))
    return result.reshape(ROWS, D)
```

```python
import jax
import jax.numpy as jnp
from jax import lax
from jax.experimental import pallas as pl
from jax.experimental.pallas import tpu as pltpu
from jax.sharding import PartitionSpec as P

MESH = pl.DeviceIdType.MESH
DH = 128
D = 1024
PAGE = 128
LAYERS = 2
USERS = 2
PAGES = 16
NY = 4
NZ = 8
NX = 4
HEADS = 8
BLOCK = 256
C = 8
ZERO = NZ * C
REQ = 16
OFFSETS = (4, 3, 5, 2, 6, 1, 7, 0)
F32 = jnp.float32
BF16 = jnp.bfloat16


def half_silu(t):
    return t * jnp.tanh(t) + t


def kernel(
    src,
    recip,
    cand,
    w_in,
    w_out,
    req_out,
    pool,
    out,
    *scratch,
):
    (
        arr,
        pack,
        rows_all,
        w_all,
        gate_send,
        gate_recv,
        att_send,
        att_recv,
    ) = [scratch[2 * i : 2 * i + 2] for i in range(8)]
    ybuf = scratch[16:32]
    (
        q_buf,
        k_buf,
        v_buf,
        acc,
        state,
        req_in,
        req_smem,
        y_ssem,
        y_rsem,
        z_ssem,
        z_rsem,
        req_ssem,
        req_rsem,
        smem_sem,
        row_ssem,
        row_fsem,
        row_rsem,
        w_ssem,
        w_fsem,
        w_rsem,
        gate_ssem,
        gate_rsem,
        att_ssem,
        att_rsem,
    ) = scratch[32:]

    me_c = lax.axis_index("cache")
    me_h = lax.axis_index("head")
    my_y = me_c // NZ
    my_z = lax.rem(me_c, NZ)
    my_x = me_h // 2
    core = lax.rem(me_h, 2)
    sibling = my_x * 2 + (1 - core)

    def y_peer(dy):
        return lax.rem(my_y + dy, NY)

    def z_peer(dz):
        return lax.rem(my_z + dz, NZ)

    def head_peer(dx, dcore):
        return lax.rem(my_x + dx, NX) * 2 + lax.rem(core + dcore, 2)

    head_steps = [(dx, dc) for dx in range(NX) for dc in range(2) if (dx, dc) != (0, 0)]

    barrier = pltpu.get_barrier_semaphore()
    for dy in range(1, NY):
        pl.semaphore_signal(
            barrier, inc=1, device_id=(y_peer(dy) * NZ + my_z, me_h), device_id_type=MESH
        )
    for dz in range(1, NZ):
        pl.semaphore_signal(
            barrier, inc=1, device_id=(my_y * NZ + z_peer(dz), me_h), device_id_type=MESH
        )
    for dx, dc in head_steps:
        pl.semaphore_signal(
            barrier, inc=1, device_id=(me_c, head_peer(dx, dc)), device_id_type=MESH
        )

    def remote(src_ref, dst_ref, send, recv, cache, head):
        return pltpu.make_async_remote_copy(
            src_ref=src_ref,
            dst_ref=dst_ref,
            send_sem=send,
            recv_sem=recv,
            device_id=(cache, head),
            device_id_type=MESH,
        )

    def y_copy(layer, i, dy):
        group = y_peer(dy) * NZ + z_peer(OFFSETS[i])
        return remote(
            pool.at[group, :, layer],
            ybuf[layer * NZ + i].at[pl.ds(my_y * 2, 2)],
            y_ssem.at[layer, i, dy],
            y_rsem.at[layer, i, my_y],
            y_peer(dy) * NZ + my_z,
            me_h,
        )

    def y_local(layer, i):
        group = my_y * NZ + z_peer(OFFSETS[i])
        return pltpu.make_async_copy(
            pool.at[group, :, layer],
            ybuf[layer * NZ + i].at[pl.ds(my_y * 2, 2)],
            y_rsem.at[layer, i, my_y],
        )

    def y_start(layer, i):
        for dy in (2, 1, 3):
            y_copy(layer, i, dy).start()
        y_local(layer, i).start()

    def y_wait(layer, i):
        for dy in range(1, NY):
            other = y_peer(dy)
            place = ybuf[layer * NZ + i].at[pl.ds(other * 2, 2)]
            remote(
                place,
                place,
                y_ssem.at[layer, i, dy],
                y_rsem.at[layer, i, other],
                other * NZ + my_z,
                me_h,
            ).wait_recv()
        y_local(layer, i).wait()

    def z_copy(layer, i):
        column = z_peer(OFFSETS[i])
        return remote(
            pack[layer].at[i],
            arr[layer].at[pl.ds(my_z * C, C)],
            z_ssem.at[layer, i],
            z_rsem.at[layer, my_z],
            my_y * NZ + column,
            me_h,
        )

    def z_wait(layer, dz):
        column = z_peer(dz)
        place = arr[layer].at[pl.ds(column * C, C)]
        remote(
            place,
            place,
            z_ssem.at[layer, 0],
            z_rsem.at[layer, column],
            my_y * NZ + column,
            me_h,
        ).wait_recv()

    def pack_send(layer, i):
        y_wait(layer, i)
        column = z_peer(OFFSETS[i])
        buf = ybuf[layer * NZ + i]
        for j in range(C):
            page = buf[req_smem[column, 0, j]]
            if OFFSETS[i] == 0:
                arr[layer][my_z * C + j] = page
            else:
                pack[layer][i, j] = page
        if OFFSETS[i] != 0:
            z_copy(layer, i).start()

    def rows_start(layer):
        place = rows_all[layer].at[me_h]
        for dx in (2, 1, 3):
            remote(
                place,
                place,
                row_ssem.at[layer, dx],
                row_rsem.at[layer, me_h],
                me_c,
                head_peer(dx, 0),
            ).start()
        remote(
            place, place, row_ssem.at[layer, 0], row_rsem.at[layer, me_h], me_c, sibling
        ).start()

    def rows_wait(layer):
        for dx in (1, 3, 2):
            source = head_peer(dx, 0)
            place = rows_all[layer].at[source]
            copy = remote(
                place, place, row_fsem.at[layer, dx], row_rsem.at[layer, source], me_c, sibling
            )
            copy.wait_recv()
            copy.start()
        for dx in (0, 1, 3, 2):
            source = head_peer(dx, 1)
            place = rows_all[layer].at[source]
            remote(
                place, place, row_fsem.at[layer, dx], row_rsem.at[layer, source], me_c, sibling
            ).wait_recv()

    def rows_drain(layer):
        place = rows_all[layer].at[me_h]
        for dx in range(NX):
            remote(
                place, place, row_ssem.at[layer, dx], row_rsem.at[layer, me_h], me_c, sibling
            ).wait_send()
        for dx in range(1, NX):
            remote(
                place, place, row_fsem.at[layer, dx], row_rsem.at[layer, me_h], me_c, sibling
            ).wait_send()

    def w_place(layer, source):
        return w_all[layer].at[source]

    def w_start():
        for layer in range(LAYERS):
            for dx in (2, 1, 3):
                remote(
                    w_out.at[layer],
                    w_place(layer, me_h),
                    w_ssem.at[layer, dx],
                    w_rsem.at[layer, me_h],
                    me_c,
                    head_peer(dx, 0),
                ).start()
            remote(
                w_out.at[layer],
                w_place(layer, me_h),
                w_ssem.at[layer, 0],
                w_rsem.at[layer, me_h],
                me_c,
                sibling,
            ).start()
            w_all[layer][me_h] = w_out[layer]

    def w_forward(layer):
        for dx in (1, 3, 2):
            source = head_peer(dx, 0)
            place = w_place(layer, source)
            copy = remote(
                place, place, w_fsem.at[layer, dx], w_rsem.at[layer, source], me_c, sibling
            )
            copy.wait_recv()
            copy.start()

    def w_wait(layer):
        for dx in range(NX):
            source = head_peer(dx, 1)
            place = w_place(layer, source)
            remote(
                place, place, w_fsem.at[layer, dx], w_rsem.at[layer, source], me_c, sibling
            ).wait_recv()

    def w_drain(layer):
        place = w_place(layer, me_h)
        for dx in range(NX):
            remote(
                place, place, w_ssem.at[layer, dx], w_rsem.at[layer, me_h], me_c, sibling
            ).wait_send()
        for dx in range(1, NX):
            remote(
                place, place, w_fsem.at[layer, dx], w_rsem.at[layer, me_h], me_c, sibling
            ).wait_send()

    def norm_rows(layer):
        xf = state[...]
        normed = xf * lax.rsqrt(jnp.mean(xf * xf, axis=-1, keepdims=True) + 1e-06)
        rows_all[layer][me_h] = normed.astype(BF16)

    def project(layer):
        def body(i, carry):
            act = jnp.dot(rows_all[layer][i], w_in[layer], preferred_element_type=F32)
            act = half_silu(act * 0.5).astype(BF16)
            gate_send[layer][i] = act[:, :DH]
            v_buf[i] = act[:, DH : 2 * DH]
            q_buf[i] = act[:, 2 * DH : 3 * DH]
            k_buf[i] = act[:, 3 * DH :]
            return carry

        lax.fori_loop(0, HEADS, body, 0)

    def gate_copy(layer, dx, dc, index):
        peer = head_peer(dx, dc)
        return remote(
            gate_send[layer].at[peer],
            gate_recv[layer].at[me_h],
            gate_ssem.at[layer, index],
            gate_rsem.at[layer, me_h],
            me_c,
            peer,
        )

    def gate_start(layer):
        for index, (dx, dc) in enumerate(head_steps):
            gate_copy(layer, dx, dc, index).start()
        gate_recv[layer][me_h] = gate_send[layer][me_h]

    def att_copy(layer, peer):
        return remote(
            att_send[layer].at[peer],
            att_recv[layer].at[me_h],
            att_ssem.at[layer, peer],
            att_rsem.at[layer, me_h],
            me_c,
            peer,
        )

    def attend(layer, user):
        per_user = HEADS // USERS
        acc[...] = jnp.zeros_like(acc)

        def body(i, carry):
            first = arr[layer][src[user * PAGES + 2 * i]]
            second = arr[layer][src[user * PAGES + 2 * i + 1]]
            keys = jnp.concatenate([first[:, :DH], second[:, :DH]], axis=0)
            values = jnp.concatenate([first[:, DH:], second[:, DH:]], axis=0)
            for r in range(per_user):
                score = lax.dot_general(
                    q_buf[user * per_user + r],
                    keys,
                    (((1,), (1,)), ((), ())),
                    preferred_element_type=F32,
                )
                weights = half_silu(score * (0.5 * DH**-0.5)).astype(BF16)
                acc[r] += jnp.dot(weights, values, preferred_element_type=F32)
            return carry

        lax.fori_loop(0, PAGES // 2, body, 0)
        scale = recip[user]
        for r in range(per_user):
            block = user * per_user + r
            own = jnp.sum(
                q_buf[block].astype(F32) * k_buf[block].astype(F32), axis=-1, keepdims=True
            )
            own = half_silu(own * (0.5 * DH**-0.5))
            total = (acc[r] + own * v_buf[block].astype(F32)) * scale
            att_send[layer][block] = total.astype(BF16)
        for r in range(per_user):
            block = user * per_user + r

            @pl.when(block != me_h)
            def _():
                att_copy(layer, block).start()

            @pl.when(block == me_h)
            def _():
                att_recv[layer][block] = att_send[layer][block]

    def finish(layer):
        for dx, dc in head_steps:
            source = head_peer(dx, dc)
            place = att_recv[layer].at[source]
            remote(
                place, place, att_ssem.at[layer, source], att_rsem.at[layer, source], me_c, source
            ).wait_recv()
            place = gate_recv[layer].at[source]
            remote(
                place, place, gate_ssem.at[layer, 0], gate_rsem.at[layer, source], me_c, source
            ).wait_recv()
        att = [att_recv[layer][h].astype(F32) for h in range(HEADS)]
        first = sum([jnp.sum(a, axis=-1, keepdims=True) for a in att]) * (1.0 / D)
        second = sum([jnp.sum(a * a, axis=-1, keepdims=True) for a in att]) * (1.0 / D)
        rstd = lax.rsqrt(second - first * first + 1e-05)
        update = state[...]
        for h in range(0, HEADS, 2):
            pair = [
                ((att[i] - first) * rstd * gate_recv[layer][i].astype(F32)).astype(BF16)
                for i in (h, h + 1)
            ]
            w_pair = jnp.concatenate([w_all[layer][h], w_all[layer][h + 1]], axis=0)
            update = update + jnp.dot(
                jnp.concatenate(pair, axis=1), w_pair, preferred_element_type=F32
            )
        return update

    def drain(layer):
        for i in range(NZ):
            for dy in range(1, NY):
                y_copy(layer, i, dy).wait_send()
            if OFFSETS[i] != 0:
                z_copy(layer, i).wait_send()
        rows_drain(layer)
        w_drain(layer)
        for index, (dx, dc) in enumerate(head_steps):
            gate_copy(layer, dx, dc, index).wait_send()
            att_copy(layer, head_peer(dx, dc)).wait_send()

    state[...] = cand[...].astype(F32)
    norm_rows(0)
    for layer in range(LAYERS):
        arr[layer][ZERO] = jnp.zeros((PAGE, 2 * DH), BF16)
    pl.semaphore_wait(barrier, NY - 1 + NZ - 1 + len(head_steps))

    def req_copy(dz):
        column = z_peer(dz)
        return remote(
            req_out.at[column],
            req_in.at[my_z],
            req_ssem.at[dz],
            req_rsem.at[my_z],
            my_y * NZ + column,
            me_h,
        )

    y_start(0, 0)
    for dz in range(1, NZ):
        req_copy(dz).start()
    req_in[my_z] = req_out[my_z]
    for i in range(1, NZ):
        y_start(0, i)
    rows_start(0)
    w_start()
    for dz in range(1, NZ):
        column = z_peer(dz)
        place = req_in.at[column]
        remote(
            place, place, req_ssem.at[dz], req_rsem.at[column], my_y * NZ + column, me_h
        ).wait_recv()
    to_smem = pltpu.make_async_copy(req_in, req_smem, smem_sem)
    to_smem.start()
    to_smem.wait()

    for i in range(NZ):
        pack_send(0, i)
        y_start(1, i)
    rows_wait(0)
    project(0)
    gate_start(0)
    for layer in range(LAYERS):
        w_forward(layer)
    for i in range(NZ):
        pack_send(1, i)
    for layer in range(LAYERS):
        for dz in range(1, NZ):
            z_wait(layer, dz)
        attend(layer, 0)
        attend(layer, 1)
        w_wait(layer)
        update = finish(layer)
        if layer + 1 < LAYERS:
            state[...] = update.astype(BF16).astype(F32)
            norm_rows(layer + 1)
            rows_start(layer + 1)
            rows_wait(layer + 1)
            project(layer + 1)
            gate_start(layer + 1)
        else:
            out[...] = update.astype(BF16)
    for layer in range(LAYERS):
        drain(layer)
    for dz in range(1, NZ):
        req_copy(dz).wait_send()


def both(shape, dtype=BF16):
    return [pltpu.VMEM(shape, dtype)] * LAYERS


def run(src, recip, cand, w_in, w_out, req, pool):
    dma = pltpu.SemaphoreType.DMA
    smem = pl.BlockSpec(memory_space=pltpu.SMEM)
    vmem = pl.BlockSpec(memory_space=pltpu.VMEM)
    return pl.pallas_call(
        kernel,
        out_shape=jax.ShapeDtypeStruct((BLOCK, D), BF16),
        in_specs=[smem, smem, vmem, vmem, vmem, vmem, pl.BlockSpec(memory_space=pl.ANY)],
        out_specs=vmem,
        scratch_shapes=[
            *both((NZ * C + 1, PAGE, 2 * DH)),
            *both((NZ - 1, C, PAGE, 2 * DH)),
            *both((HEADS, BLOCK, D)),
            *both((HEADS, DH, D)),
            *both((HEADS, BLOCK, DH)),
            *both((HEADS, BLOCK, DH)),
            *both((HEADS, BLOCK, DH)),
            *both((HEADS, BLOCK, DH)),
            *[pltpu.VMEM((2 * NY, PAGE, 2 * DH), BF16)] * (LAYERS * NZ),
            pltpu.VMEM((HEADS, BLOCK, DH), BF16),
            pltpu.VMEM((HEADS, BLOCK, DH), BF16),
            pltpu.VMEM((HEADS, BLOCK, DH), BF16),
            pltpu.VMEM((HEADS // USERS, BLOCK, DH), F32),
            pltpu.VMEM((BLOCK, D), F32),
            pltpu.VMEM((NZ, 1, 128), jnp.int32),
            pltpu.SMEM((NZ, 1, 128), jnp.int32),
            dma((LAYERS, NZ, NY)),
            dma((LAYERS, NZ, NY)),
            dma((LAYERS, NZ)),
            dma((LAYERS, NZ)),
            dma((NZ,)),
            dma((NZ,)),
            dma,
            dma((LAYERS, NX)),
            dma((LAYERS, NX)),
            dma((LAYERS, HEADS)),
            dma((LAYERS, NX)),
            dma((LAYERS, NX)),
            dma((LAYERS, HEADS)),
            dma((LAYERS, HEADS)),
            dma((LAYERS, HEADS)),
            dma((LAYERS, HEADS)),
            dma((LAYERS, HEADS)),
        ],
        compiler_params=pltpu.CompilerParams(
            collective_id=0, has_side_effects=True, vmem_limit_bytes=62 * 2**20
        ),
    )(src, recip, cand, w_in, w_out, req, pool)


def shards(candidates, proj_in, proj_out, page_pool, page_owner, history_pages):
    owners = page_owner.reshape(-1)
    count = owners.shape[0]
    order = jnp.arange(count)
    before = order[None, :] < order[:, None]
    slots = jnp.sum(((owners[:, None] == owners[None, :]) & before).astype(jnp.int32), axis=1)
    live = (jnp.arange(PAGES)[None, :] < history_pages[:, None]).reshape(-1)
    column = owners % NZ
    rank = jnp.sum(
        ((column[:, None] == column[None, :]) & before & live[None, :]).astype(jnp.int32), axis=1
    )
    place = (owners // NZ) * 2 + slots
    src = jnp.where(live, column * C + rank, ZERO).astype(jnp.int32)
    chosen = (src[None, :] == jnp.arange(NZ * C)[:, None]).astype(jnp.int32)
    req = jnp.sum(chosen * place[None, :], axis=1).reshape(NZ, 1, C)
    req = jnp.pad(req, ((0, 0), (0, 0), (0, 128 - C))).astype(jnp.int32)
    recip = 1.0 / (history_pages * PAGE + 1).astype(F32)
    return run(src, recip, candidates, proj_in, proj_out, req, page_pool[0])


def solution(mesh):
    return jax.shard_map(
        shards,
        mesh=mesh,
        in_specs=(
            P(("cache", "head"), None),
            P(None, None, "head"),
            P(None, "head", None),
            P("cache", None, None, None, None, "head"),
            P("cache", None, None),
            P("cache"),
        ),
        out_specs=P(("cache", "head"), None),
        check_vma=False,
    )
```

```python
import functools

import jax
import jax.numpy as jnp
from jax import lax
from jax.experimental import pallas as pl
from jax.experimental.pallas import tpu as pltpu
from jax.sharding import PartitionSpec as P

MESH = pl.DeviceIdType.MESH
DH = 128
D = 1024
PAGE = 128
LAYERS = 2
USERS = 2
PAGES = 16
NY = 4
NZ = 8
NX = 4
HEADS = 8
BLOCK = 256
CAPS = (6, 8)
WINDOW = 3
OFFSETS = (4, 3, 5, 2, 6, 1, 7, 0)
F32 = jnp.float32
BF16 = jnp.bfloat16


def half_silu(t):
    return t * jnp.tanh(t) + t


def kernel(
    C,
    lengths,
    owners,
    cand,
    w_in,
    w_out,
    pool,
    out,
    overflow,
    *scratch,
):
    (
        arr,
        pack,
        rows_all,
        w_all,
        gate_send,
        gate_recv,
        att_send,
        att_recv,
    ) = [scratch[2 * i : 2 * i + 2] for i in range(8)]
    ybuf = scratch[16:32]
    (
        q_buf,
        k_buf,
        v_buf,
        acc,
        state,
        req_out,
        req_in,
        req_smem,
        src_vmem,
        src,
        flag_out,
        flag_in,
        flag_all,
        flag_smem,
        y_ssem,
        y_rsem,
        z_ssem,
        z_rsem,
        req_ssem,
        req_rsem,
        flag_ssem,
        flag_rsem,
        smem_sem,
        row_ssem,
        row_fsem,
        row_rsem,
        w_ssem,
        w_fsem,
        w_rsem,
        gate_ssem,
        gate_rsem,
        att_ssem,
        att_rsem,
    ) = scratch[32:]

    ZERO = NZ * C
    me_c = lax.axis_index("cache")
    me_h = lax.axis_index("head")
    my_y = me_c // NZ
    my_z = lax.rem(me_c, NZ)
    my_x = me_h // 2
    core = lax.rem(me_h, 2)
    sibling = my_x * 2 + (1 - core)

    def y_peer(dy):
        return lax.rem(my_y + dy, NY)

    def z_peer(dz):
        return lax.rem(my_z + dz, NZ)

    def head_peer(dx, dcore):
        return lax.rem(my_x + dx, NX) * 2 + lax.rem(core + dcore, 2)

    head_steps = [(dx, dc) for dx in range(NX) for dc in range(2) if (dx, dc) != (0, 0)]

    barrier = pltpu.get_barrier_semaphore()
    for dy in range(1, NY):
        pl.semaphore_signal(
            barrier, inc=1, device_id=(y_peer(dy) * NZ + my_z, me_h), device_id_type=MESH
        )
    for dz in range(1, NZ):
        pl.semaphore_signal(
            barrier, inc=1, device_id=(my_y * NZ + z_peer(dz), me_h), device_id_type=MESH
        )
    for dx, dc in head_steps:
        pl.semaphore_signal(
            barrier, inc=1, device_id=(me_c, head_peer(dx, dc)), device_id_type=MESH
        )

    def remote(src_ref, dst_ref, send, recv, cache, head):
        return pltpu.make_async_remote_copy(
            src_ref=src_ref,
            dst_ref=dst_ref,
            send_sem=send,
            recv_sem=recv,
            device_id=(cache, head),
            device_id_type=MESH,
        )

    def wait_bytes(ref, sem):
        pltpu.make_async_copy(ref, ref, sem).wait()

    def y_start(n):
        layer, i = divmod(n, NZ)
        column = z_peer(OFFSETS[i])
        place = ybuf[n].at[pl.ds(my_y * 2, 2)]
        for dy in (2, 1, 3):
            remote(
                pool.at[y_peer(dy) * NZ + column, :, layer],
                place,
                y_ssem.at[layer],
                y_rsem.at[n],
                y_peer(dy) * NZ + my_z,
                me_h,
            ).start()
        pltpu.make_async_copy(
            pool.at[my_y * NZ + column, :, layer], place, y_rsem.at[n]
        ).start()

    def pack_send(n):
        if n + WINDOW < LAYERS * NZ:
            y_start(n + WINDOW)
        layer, i = divmod(n, NZ)
        wait_bytes(ybuf[n], y_rsem.at[n])
        column = z_peer(OFFSETS[i])
        for j in range(C):
            page = ybuf[n][jnp.clip(req_smem[column, 0, j], 0, 2 * NY - 1)]
            if OFFSETS[i] == 0:
                arr[layer][my_z * C + j] = page
            else:
                pack[layer][i, j] = page
        if OFFSETS[i] != 0:
            remote(
                pack[layer].at[i],
                arr[layer].at[pl.ds(my_z * C, C)],
                z_ssem.at[layer],
                z_rsem.at[layer],
                my_y * NZ + column,
                me_h,
            ).start()

    def z_wait(layer):
        wait_bytes(arr[layer].at[pl.ds(0, (NZ - 1) * C)], z_rsem.at[layer])

    def rows_start(layer):
        place = rows_all[layer].at[me_h]
        for dx in (2, 1, 3):
            remote(
                place,
                place,
                row_ssem.at[layer, dx],
                row_rsem.at[layer, me_h],
                me_c,
                head_peer(dx, 0),
            ).start()
        remote(
            place, place, row_ssem.at[layer, 0], row_rsem.at[layer, me_h], me_c, sibling
        ).start()

    def rows_wait(layer):
        for dx in (1, 3, 2):
            source = head_peer(dx, 0)
            place = rows_all[layer].at[source]
            copy = remote(
                place, place, row_fsem.at[layer, dx], row_rsem.at[layer, source], me_c, sibling
            )
            copy.wait_recv()
            copy.start()
        for dx in (0, 1, 3, 2):
            source = head_peer(dx, 1)
            place = rows_all[layer].at[source]
            remote(
                place, place, row_fsem.at[layer, dx], row_rsem.at[layer, source], me_c, sibling
            ).wait_recv()

    def rows_drain(layer):
        place = rows_all[layer].at[me_h]
        for dx in range(NX):
            remote(
                place, place, row_ssem.at[layer, dx], row_rsem.at[layer, me_h], me_c, sibling
            ).wait_send()
        for dx in range(1, NX):
            remote(
                place, place, row_fsem.at[layer, dx], row_rsem.at[layer, me_h], me_c, sibling
            ).wait_send()

    def w_place(layer, source):
        return w_all[layer].at[source]

    def w_start():
        for layer in range(LAYERS):
            for dx in (2, 1, 3):
                remote(
                    w_out.at[layer],
                    w_place(layer, me_h),
                    w_ssem.at[layer, dx],
                    w_rsem.at[layer, me_h],
                    me_c,
                    head_peer(dx, 0),
                ).start()
            remote(
                w_out.at[layer],
                w_place(layer, me_h),
                w_ssem.at[layer, 0],
                w_rsem.at[layer, me_h],
                me_c,
                sibling,
            ).start()
            w_all[layer][me_h] = w_out[layer]

    def w_forward(layer):
        for dx in (1, 3, 2):
            source = head_peer(dx, 0)
            place = w_place(layer, source)
            copy = remote(
                place, place, w_fsem.at[layer, dx], w_rsem.at[layer, source], me_c, sibling
            )
            copy.wait_recv()
            copy.start()

    def w_wait(layer):
        for dx in range(NX):
            source = head_peer(dx, 1)
            place = w_place(layer, source)
            remote(
                place, place, w_fsem.at[layer, dx], w_rsem.at[layer, source], me_c, sibling
            ).wait_recv()

    def w_drain(layer):
        place = w_place(layer, me_h)
        for dx in range(NX):
            remote(
                place, place, w_ssem.at[layer, dx], w_rsem.at[layer, me_h], me_c, sibling
            ).wait_send()
        for dx in range(1, NX):
            remote(
                place, place, w_fsem.at[layer, dx], w_rsem.at[layer, me_h], me_c, sibling
            ).wait_send()

    def norm_rows(layer):
        xf = state[...]
        normed = xf * lax.rsqrt(jnp.mean(xf * xf, axis=-1, keepdims=True) + 1e-06)
        rows_all[layer][me_h] = normed.astype(BF16)

    def project(layer):
        def body(i, carry):
            act = jnp.dot(rows_all[layer][i], w_in[layer], preferred_element_type=F32)
            act = half_silu(act * 0.5).astype(BF16)
            gate_send[layer][i] = act[:, :DH]
            v_buf[i] = act[:, DH : 2 * DH]
            q_buf[i] = act[:, 2 * DH : 3 * DH]
            k_buf[i] = act[:, 3 * DH :]
            return carry

        lax.fori_loop(0, HEADS, body, 0)

    def gate_start(layer):
        for dx, dc in head_steps:
            peer = head_peer(dx, dc)
            remote(
                gate_send[layer].at[peer],
                gate_recv[layer].at[me_h],
                gate_ssem.at[layer],
                gate_rsem.at[layer],
                me_c,
                peer,
            ).start()
        gate_recv[layer][me_h] = gate_send[layer][me_h]

    def att_copy(layer, peer):
        return remote(
            att_send[layer].at[peer],
            att_recv[layer].at[me_h],
            att_ssem.at[layer],
            att_rsem.at[layer],
            me_c,
            peer,
        )

    def attend(layer, user):
        per_user = HEADS // USERS
        acc[...] = jnp.zeros_like(acc)

        def body(i, carry):
            first, second = [
                arr[layer][jnp.clip(src[user * PAGES + 2 * i + k, 0], 0, ZERO)] for k in (0, 1)
            ]
            keys = jnp.concatenate([first[:, :DH], second[:, :DH]], axis=0)
            values = jnp.concatenate([first[:, DH:], second[:, DH:]], axis=0)
            for r in range(per_user):
                score = lax.dot_general(
                    q_buf[user * per_user + r],
                    keys,
                    (((1,), (1,)), ((), ())),
                    preferred_element_type=F32,
                )
                weights = half_silu(score * (0.5 * DH**-0.5)).astype(BF16)
                acc[r] += jnp.dot(weights, values, preferred_element_type=F32)
            return carry

        lax.fori_loop(0, PAGES // 2, body, 0)
        scale = 1.0 / jnp.full((1, DH), lengths[user] * PAGE + 1, jnp.int32).astype(F32)
        for r in range(per_user):
            block = user * per_user + r
            own = jnp.sum(
                q_buf[block].astype(F32) * k_buf[block].astype(F32), axis=-1, keepdims=True
            )
            own = half_silu(own * (0.5 * DH**-0.5))
            total = (acc[r] + own * v_buf[block].astype(F32)) * scale
            att_send[layer][block] = total.astype(BF16)
        for r in range(per_user):
            block = user * per_user + r

            @pl.when(block != me_h)
            def _():
                att_copy(layer, block).start()

            @pl.when(block == me_h)
            def _():
                att_recv[layer][block] = att_send[layer][block]

    def finish(layer):
        wait_bytes(gate_recv[layer].at[pl.ds(0, HEADS - 1)], gate_rsem.at[layer])
        wait_bytes(att_recv[layer].at[pl.ds(0, HEADS - 1)], att_rsem.at[layer])
        att = [att_recv[layer][h].astype(F32) for h in range(HEADS)]
        first = sum([jnp.sum(a, axis=-1, keepdims=True) for a in att]) * (1.0 / D)
        second = sum([jnp.sum(a * a, axis=-1, keepdims=True) for a in att]) * (1.0 / D)
        rstd = lax.rsqrt(second - first * first + 1e-05)
        update = state[...]
        for h in range(0, HEADS, 2):
            pair = [
                ((att[i] - first) * rstd * gate_recv[layer][i].astype(F32)).astype(BF16)
                for i in (h, h + 1)
            ]
            w_pair = jnp.concatenate([w_all[layer][h], w_all[layer][h + 1]], axis=0)
            update = update + jnp.dot(
                jnp.concatenate(pair, axis=1), w_pair, preferred_element_type=F32
            )
        return update

    def drain(layer):
        wait_bytes(gate_send[layer].at[pl.ds(0, HEADS - 1)], gate_ssem.at[layer])
        wait_bytes(att_send[layer].at[pl.ds(0, HEADS - 1)], att_ssem.at[layer])
        wait_bytes(arr[layer].at[pl.ds(0, NZ * (NY - 1) * 2)], y_ssem.at[layer])
        wait_bytes(pack[layer], z_ssem.at[layer])
        rows_drain(layer)
        w_drain(layer)

    def make_requests():
        count = USERS * PAGES
        lane = lax.broadcasted_iota(jnp.int32, (count, count), 1)
        sub = lax.broadcasted_iota(jnp.int32, (count, count), 0)
        before = lane < sub
        row = jnp.zeros((1, count), jnp.int32)
        col = jnp.zeros((count, 1), jnp.int32)
        for p in range(count):
            owner = owners[p // PAGES, 0, p % PAGES]
            row = jnp.where(lane[:1] == p, owner, row)
            col = jnp.where(sub[:, :1] == p, owner, col)

        def live_of(index):
            length = jnp.where(index < PAGES, lengths[0], lengths[1])
            return lax.rem(index, PAGES) < length

        def total(mask, axis):
            return jnp.sum(mask.astype(jnp.int32), axis=axis, keepdims=True)

        slot = jnp.minimum(total((row == col) & before, 1), 1)
        near = (lax.rem(row, NZ) == lax.rem(col, NZ)) & before & live_of(lane)
        rank = total(near, 1)
        live = live_of(lax.broadcasted_iota(jnp.int32, (count, 1), 0))
        place = lax.rem(col // NZ, NY) * 2 + slot
        target = jnp.where(live & (rank < C), lax.rem(col, NZ) * C + rank, ZERO)
        src_vmem[...] = jnp.broadcast_to(target, (count, 128))
        over = jnp.max((live & (rank >= C)).astype(jnp.int32), axis=0, keepdims=True)
        lanes = lax.broadcasted_iota(jnp.int32, (count, 128), 1)
        for z in range(NZ):
            hit = (target == lanes + z * C) & (target < ZERO) & (lanes < C)
            line = jnp.sum(jnp.where(hit, place, 0), axis=0, keepdims=True)
            line = jnp.where(lanes[:1] == 127, over, line)
            req_out[z] = line

    state[...] = cand[...].astype(F32)
    norm_rows(0)
    make_requests()
    for layer in range(LAYERS):
        arr[layer][ZERO] = jnp.zeros((PAGE, 2 * DH), BF16)
    pl.semaphore_wait(barrier, NY - 1 + NZ - 1 + len(head_steps))

    y_start(0)
    for dz in range(1, NZ):
        column = z_peer(dz)
        remote(
            req_out.at[column],
            req_in.at[my_z],
            req_ssem,
            req_rsem,
            my_y * NZ + column,
            me_h,
        ).start()
    req_in[my_z] = req_out[my_z]
    for n in range(1, WINDOW):
        y_start(n)
    rows_start(0)
    src_copy = pltpu.make_async_copy(src_vmem, src, smem_sem.at[1])
    src_copy.start()
    wait_bytes(req_in.at[pl.ds(0, NZ - 1)], req_rsem)
    to_smem = pltpu.make_async_copy(req_in, req_smem, smem_sem.at[0])
    to_smem.start()
    flag_out[0] = jnp.max(req_in[...], axis=0)
    for dy in range(1, NY):
        remote(
            flag_out.at[0],
            flag_in.at[my_y],
            flag_ssem,
            flag_rsem,
            y_peer(dy) * NZ + my_z,
            me_h,
        ).start()
    flag_in[my_y] = flag_out[0]
    to_smem.wait()
    src_copy.wait()

    for n in range(6):
        pack_send(n)
    rows_wait(0)
    project(0)
    gate_start(0)
    w_start()
    for n in range(6, 11):
        pack_send(n)
    for layer in range(LAYERS):
        w_forward(layer)
    pack_send(11)
    z_wait(0)
    attend(0, 0)
    attend(0, 1)
    pack_send(12)
    for layer in range(LAYERS):
        w_wait(layer)
    update = finish(0)
    state[...] = update.astype(BF16).astype(F32)
    norm_rows(1)
    rows_start(1)
    for n in range(13, 15):
        pack_send(n)
    rows_wait(1)
    project(1)
    gate_start(1)
    pack_send(15)
    drain(0)
    wait_bytes(req_in.at[pl.ds(0, NZ - 1)], req_ssem)
    wait_bytes(flag_in.at[pl.ds(0, NY - 1)], flag_rsem)
    wait_bytes(flag_in.at[pl.ds(0, NY - 1)], flag_ssem)
    flag_all[...] = jnp.max(flag_in[...], axis=0)
    to_smem = pltpu.make_async_copy(flag_all, flag_smem, smem_sem.at[0])
    to_smem.start()
    to_smem.wait()
    overflow[0] = flag_smem[0, 127]
    z_wait(1)
    attend(1, 0)
    attend(1, 1)
    out[...] = finish(1).astype(BF16)
    drain(1)


def both(shape, dtype=BF16):
    return [pltpu.VMEM(shape, dtype)] * LAYERS


def run(turn, lengths, owners, cand, w_in, w_out, pool):
    C = CAPS[turn]
    dma = pltpu.SemaphoreType.DMA
    vmem = pl.BlockSpec(memory_space=pltpu.VMEM)
    smem = pl.BlockSpec(memory_space=pltpu.SMEM)
    return pl.pallas_call(
        functools.partial(kernel, C),
        out_shape=(
            jax.ShapeDtypeStruct((BLOCK, D), BF16),
            jax.ShapeDtypeStruct((1,), jnp.int32),
        ),
        in_specs=[
            smem,
            smem,
            vmem,
            vmem,
            vmem,
            pl.BlockSpec(memory_space=pl.ANY),
        ],
        out_specs=(vmem, smem),
        scratch_shapes=[
            *both((NZ * C + 1, PAGE, 2 * DH)),
            *both((NZ - 1, C, PAGE, 2 * DH)),
            *both((HEADS, BLOCK, D)),
            *both((HEADS, DH, D)),
            *both((HEADS, BLOCK, DH)),
            *both((HEADS, BLOCK, DH)),
            *both((HEADS, BLOCK, DH)),
            *both((HEADS, BLOCK, DH)),
            *[pltpu.VMEM((2 * NY, PAGE, 2 * DH), BF16)] * (LAYERS * NZ),
            pltpu.VMEM((HEADS, BLOCK, DH), BF16),
            pltpu.VMEM((HEADS, BLOCK, DH), BF16),
            pltpu.VMEM((HEADS, BLOCK, DH), BF16),
            pltpu.VMEM((HEADS // USERS, BLOCK, DH), F32),
            pltpu.VMEM((BLOCK, D), F32),
            pltpu.VMEM((NZ, 1, 128), jnp.int32),
            pltpu.VMEM((NZ, 1, 128), jnp.int32),
            pltpu.SMEM((NZ, 1, 128), jnp.int32),
            pltpu.VMEM((USERS * PAGES, 128), jnp.int32),
            pltpu.SMEM((USERS * PAGES, 128), jnp.int32),
            pltpu.VMEM((1, 1, 128), jnp.int32),
            pltpu.VMEM((NY, 1, 128), jnp.int32),
            pltpu.VMEM((1, 128), jnp.int32),
            pltpu.SMEM((1, 128), jnp.int32),
            dma((LAYERS,)),
            dma((LAYERS * NZ,)),
            dma((LAYERS,)),
            dma((LAYERS,)),
            dma,
            dma,
            dma,
            dma,
            dma((2,)),
            dma((LAYERS, NX)),
            dma((LAYERS, NX)),
            dma((LAYERS, HEADS)),
            dma((LAYERS, NX)),
            dma((LAYERS, NX)),
            dma((LAYERS, HEADS)),
            dma((LAYERS,)),
            dma((LAYERS,)),
            dma((LAYERS,)),
            dma((LAYERS,)),
        ],
        compiler_params=pltpu.CompilerParams(
            collective_id=turn, has_side_effects=True, vmem_limit_bytes=62 * 2**20
        ),
    )(lengths, owners, cand, w_in, w_out, pool)


def shards(candidates, proj_in, proj_out, page_pool, page_owner, history_pages):
    owners = page_owner.transpose(0, 2, 1)
    args = (history_pages, owners, candidates, proj_in, proj_out, page_pool[0])
    first, overflow = run(0, *args)
    return lax.switch(overflow[0], [lambda: first, lambda: run(1, *args)[0]])


def solution(mesh):
    return jax.shard_map(
        shards,
        mesh=mesh,
        in_specs=(
            P(("cache", "head"), None),
            P(None, None, "head"),
            P(None, "head", None),
            P("cache", None, None, None, None, "head"),
            P("cache", None, None),
            P("cache"),
        ),
        out_specs=P(("cache", "head"), None),
        check_vma=False,
    )
```

```python
import functools

import jax
import jax.numpy as jnp
from jax import lax
from jax.experimental import pallas as pl
from jax.experimental.pallas import tpu as pltpu
from jax.sharding import PartitionSpec as P

MESH = pl.DeviceIdType.MESH
DH = 128
D = 1024
PAGE = 128
LAYERS = 2
USERS = 2
PAGES = 16
NY = 4
NZ = 8
NX = 4
HEADS = 8
BLOCK = 256
CAPS = (6, 8)
WINDOW = 3
OFFSETS = (4, 3, 5, 2, 6, 1, 7, 0)
F32 = jnp.float32
BF16 = jnp.bfloat16


def half_silu(t):
    return t * jnp.tanh(t) + t


def kernel(
    C,
    lengths,
    owners,
    cand,
    w_in,
    w_out,
    pool,
    out,
    overflow,
    *scratch,
):
    (
        arr,
        pack,
        w_all,
        gate_recv,
        q_buf,
        att_send,
        att_recv,
    ) = [scratch[2 * i : 2 * i + 2] for i in range(7)]
    ybuf = scratch[14:30]
    (
        rows_all,
        w_next,
        k_buf,
        v_buf,
        own_buf,
        out_send,
        keys,
        values,
        state,
        req_out,
        req_in,
        req_smem,
        src_vmem,
        src,
        flag_out,
        flag_in,
        flag_all,
        flag_smem,
        y_ssem,
        y_rsem,
        z_ssem,
        z_rsem,
        req_ssem,
        req_rsem,
        flag_ssem,
        flag_rsem,
        smem_sem,
        spread_ssem,
        spread_rsem,
        cross_ssem,
        cross_rsem,
        att_ssem,
        att_rsem,
    ) = scratch[30:]

    ZERO = NZ * C
    me_c = lax.axis_index("cache")
    me_h = lax.axis_index("head")
    my_y = me_c // NZ
    my_z = lax.rem(me_c, NZ)
    my_x = me_h // 2
    core = lax.rem(me_h, 2)
    sibling = my_x * 2 + (1 - core)

    def y_peer(dy):
        return lax.rem(my_y + dy, NY)

    def z_peer(dz):
        return lax.rem(my_z + dz, NZ)

    def head_peer(dx, dcore):
        return lax.rem(my_x + dx, NX) * 2 + lax.rem(core + dcore, 2)

    head_steps = [(dx, dc) for dx in range(NX) for dc in range(2) if (dx, dc) != (0, 0)]

    barrier = pltpu.get_barrier_semaphore()
    for dy in range(1, NY):
        pl.semaphore_signal(
            barrier, inc=1, device_id=(y_peer(dy) * NZ + my_z, me_h), device_id_type=MESH
        )
    for dz in range(1, NZ):
        pl.semaphore_signal(
            barrier, inc=1, device_id=(my_y * NZ + z_peer(dz), me_h), device_id_type=MESH
        )
    for dx, dc in head_steps:
        pl.semaphore_signal(
            barrier, inc=1, device_id=(me_c, head_peer(dx, dc)), device_id_type=MESH
        )

    def remote(src_ref, dst_ref, send, recv, cache, head):
        return pltpu.make_async_remote_copy(
            src_ref=src_ref,
            dst_ref=dst_ref,
            send_sem=send,
            recv_sem=recv,
            device_id=(cache, head),
            device_id_type=MESH,
        )

    def wait_bytes(ref, sem):
        pltpu.make_async_copy(ref, ref, sem).wait()

    def y_start(n):
        layer, i = divmod(n, NZ)
        column = z_peer(OFFSETS[i])
        place = ybuf[n].at[pl.ds(my_y * 2, 2)]
        for dy in (2, 1, 3):
            remote(
                pool.at[y_peer(dy) * NZ + column, :, layer],
                place,
                y_ssem.at[layer],
                y_rsem.at[n],
                y_peer(dy) * NZ + my_z,
                me_h,
            ).start()
        pltpu.make_async_copy(
            pool.at[my_y * NZ + column, :, layer], place, y_rsem.at[n]
        ).start()

    def pack_send(n):
        if n + WINDOW < LAYERS * NZ:
            y_start(n + WINDOW)
        layer, i = divmod(n, NZ)
        wait_bytes(ybuf[n], y_rsem.at[n])
        column = z_peer(OFFSETS[i])
        for j in range(C):
            page = ybuf[n][jnp.clip(req_smem[column, 0, j], 0, 2 * NY - 1)]
            if OFFSETS[i] == 0:
                arr[layer][my_z * C + j] = page
            else:
                pack[layer][i, j] = page
        if OFFSETS[i] != 0:
            remote(
                pack[layer].at[i],
                arr[layer].at[pl.ds(my_z * C, C)],
                z_ssem.at[layer],
                z_rsem.at[layer],
                my_y * NZ + column,
                me_h,
            ).start()

    def z_wait(layer):
        wait_bytes(arr[layer].at[pl.ds(0, (NZ - 1) * C)], z_rsem.at[layer])

    def spread_start(k, block, places):
        for dx in (2, 1, 3):
            remote(
                block,
                places.at[me_h],
                spread_ssem.at[k],
                spread_rsem.at[k, me_h],
                me_c,
                head_peer(dx, 0),
            ).start()
        remote(
            block, places.at[me_h], spread_ssem.at[k], spread_rsem.at[k, me_h], me_c, sibling
        ).start()

    def spread_forward(k, places):
        for dx in (1, 3, 2):
            source = head_peer(dx, 0)
            place = places.at[source]
            wait_bytes(place, spread_rsem.at[k, source])
            remote(
                place, place, spread_ssem.at[k], spread_rsem.at[k, source], me_c, sibling
            ).start()

    def spread_wait(k, places):
        for dx in (0, 1, 3, 2):
            source = head_peer(dx, 1)
            wait_bytes(places.at[source], spread_rsem.at[k, source])

    def spread_drain(k, places):
        wait_bytes(places.at[pl.ds(0, HEADS - 1)], spread_ssem.at[k])

    def normed_rows():
        xf = state[...]
        normed = xf * lax.rsqrt(jnp.mean(xf * xf, axis=-1, keepdims=True) + 1e-06)
        return normed.astype(BF16)

    def activations(rows, w):
        act = jnp.dot(rows, w, preferred_element_type=F32)
        act = half_silu(act * 0.5).astype(BF16)
        return [act[:, i * DH : (i + 1) * DH] for i in range(4)]

    def reciprocal(user):
        return 1.0 / jnp.full((1, DH), lengths[user] * PAGE + 1, jnp.int32).astype(F32)

    def own_term(query, key, value):
        own = jnp.sum(query.astype(F32) * key.astype(F32), axis=-1, keepdims=True)
        return half_silu(own * (0.5 * DH**-0.5)) * value.astype(F32)

    def project_head():
        def body(i, carry):
            gate, value, query, key = activations(rows_all[i], w_in[0])
            out_send[0, i] = gate
            v_buf[i] = value
            q_buf[0][i] = query
            k_buf[i] = key
            return carry

        lax.fori_loop(0, HEADS, body, 0)
        for dx, dc in head_steps:
            cross_copy(0, head_peer(dx, dc)).start()
        gate_recv[0][me_h] = out_send[0, me_h]

    def cross_copy(layer, peer):
        return remote(
            out_send.at[layer, peer],
            (gate_recv[0] if layer == 0 else q_buf[1]).at[me_h],
            cross_ssem.at[layer],
            cross_rsem.at[layer],
            me_c,
            peer,
        )

    def project_rows():
        rows_all[0] = normed_rows()
        scale = reciprocal(me_h // (HEADS // USERS))

        def one(head):
            gate, value, query, key = activations(rows_all[0], w_next[head])
            gate_recv[1][head] = gate
            own_buf[head] = own_term(query, key, value) * scale
            return query

        def body(step, carry):
            head = lax.rem(me_h + step, HEADS)
            out_send[1, head] = one(head)
            cross_copy(1, head).start()
            return carry

        lax.fori_loop(1, HEADS, body, 0)
        q_buf[1][me_h] = one(me_h)

    def att_copy(layer, peer):
        return remote(
            att_send[layer].at[peer],
            att_recv[layer].at[me_h],
            att_ssem.at[layer],
            att_rsem.at[layer],
            me_c,
            peer,
        )

    def attend(layer, user):
        per_user = HEADS // USERS
        for p in range(PAGES):
            page = arr[layer][jnp.clip(src[user * PAGES + p, 0], 0, ZERO)]
            keys[pl.ds(p * PAGE, PAGE)] = page[:, :DH]
            values[pl.ds(p * PAGE, PAGE)] = page[:, DH:]
        query = q_buf[layer][pl.ds(user * per_user, per_user)].reshape(per_user * BLOCK, DH)
        total = jnp.zeros((per_user * BLOCK, DH), F32)
        for e in range(0, PAGES * PAGE, 2 * PAGE):
            score = lax.dot_general(
                query,
                keys[pl.ds(e, 2 * PAGE)],
                (((1,), (1,)), ((), ())),
                preferred_element_type=F32,
            )
            weights = half_silu(score * (0.5 * DH**-0.5)).astype(BF16)
            total = total + jnp.dot(
                weights, values[pl.ds(e, 2 * PAGE)], preferred_element_type=F32
            )
        scale = reciprocal(user)
        for r in range(per_user):
            block = user * per_user + r
            here = total[r * BLOCK : (r + 1) * BLOCK]
            if layer == 0:
                here = here + own_term(q_buf[0][block], k_buf[block], v_buf[block])
            att_send[layer][block] = (here * scale).astype(BF16)
        for r in range(per_user):
            block = user * per_user + r

            @pl.when(block != me_h)
            def _():
                att_copy(layer, block).start()

            @pl.when(block == me_h)
            def _():
                att_recv[layer][block] = att_send[layer][block]

    def finish(layer):
        wait_bytes(att_recv[layer].at[pl.ds(0, HEADS - 1)], att_rsem.at[layer])
        att = [att_recv[layer][h].astype(F32) for h in range(HEADS)]
        if layer == 1:
            att = [att[h] + own_buf[h] for h in range(HEADS)]
        first = sum([jnp.sum(a, axis=-1, keepdims=True) for a in att]) * (1.0 / D)
        second = sum([jnp.sum(a * a, axis=-1, keepdims=True) for a in att]) * (1.0 / D)
        rstd = lax.rsqrt(second - first * first + 1e-05)
        update = state[...]
        for h in range(0, HEADS, 2):
            pair = [
                ((att[i] - first) * rstd * gate_recv[layer][i].astype(F32)).astype(BF16)
                for i in (h, h + 1)
            ]
            w_pair = jnp.concatenate([w_all[layer][h], w_all[layer][h + 1]], axis=0)
            update = update + jnp.dot(
                jnp.concatenate(pair, axis=1), w_pair, preferred_element_type=F32
            )
        return update

    def make_requests():
        count = USERS * PAGES
        lane = lax.broadcasted_iota(jnp.int32, (count, count), 1)
        sub = lax.broadcasted_iota(jnp.int32, (count, count), 0)
        before = lane < sub
        row = jnp.zeros((1, count), jnp.int32)
        col = jnp.zeros((count, 1), jnp.int32)
        for p in range(count):
            owner = owners[p // PAGES, 0, p % PAGES]
            row = jnp.where(lane[:1] == p, owner, row)
            col = jnp.where(sub[:, :1] == p, owner, col)

        def live_of(index):
            length = jnp.where(index < PAGES, lengths[0], lengths[1])
            return lax.rem(index, PAGES) < length

        def total(mask, axis):
            return jnp.sum(mask.astype(jnp.int32), axis=axis, keepdims=True)

        slot = jnp.minimum(total((row == col) & before, 1), 1)
        near = (lax.rem(row, NZ) == lax.rem(col, NZ)) & before & live_of(lane)
        rank = total(near, 1)
        live = live_of(lax.broadcasted_iota(jnp.int32, (count, 1), 0))
        place = lax.rem(col // NZ, NY) * 2 + slot
        target = jnp.where(live & (rank < C), lax.rem(col, NZ) * C + rank, ZERO)
        src_vmem[...] = jnp.broadcast_to(target, (count, 128))
        over = jnp.max((live & (rank >= C)).astype(jnp.int32), axis=0, keepdims=True)
        lanes = lax.broadcasted_iota(jnp.int32, (count, 128), 1)
        for z in range(NZ):
            hit = (target == lanes + z * C) & (target < ZERO) & (lanes < C)
            line = jnp.sum(jnp.where(hit, place, 0), axis=0, keepdims=True)
            line = jnp.where(lanes[:1] == 127, over, line)
            req_out[z] = line

    state[...] = cand[...].astype(F32)
    rows_all[me_h] = normed_rows()
    make_requests()
    for layer in range(LAYERS):
        arr[layer][ZERO] = jnp.zeros((PAGE, 2 * DH), BF16)
    pl.semaphore_wait(barrier, NY - 1 + NZ - 1 + len(head_steps))

    y_start(0)
    for dz in range(1, NZ):
        column = z_peer(dz)
        remote(
            req_out.at[column],
            req_in.at[my_z],
            req_ssem,
            req_rsem,
            my_y * NZ + column,
            me_h,
        ).start()
    req_in[my_z] = req_out[my_z]
    for n in range(1, WINDOW):
        y_start(n)
    spread_start(0, rows_all.at[me_h], rows_all)
    src_copy = pltpu.make_async_copy(src_vmem, src, smem_sem.at[1])
    src_copy.start()
    wait_bytes(req_in.at[pl.ds(0, NZ - 1)], req_rsem)
    to_smem = pltpu.make_async_copy(req_in, req_smem, smem_sem.at[0])
    to_smem.start()
    flag_out[0] = jnp.max(req_in[...], axis=0)
    for dy in range(1, NY):
        remote(
            flag_out.at[0],
            flag_in.at[my_y],
            flag_ssem,
            flag_rsem,
            y_peer(dy) * NZ + my_z,
            me_h,
        ).start()
    flag_in[my_y] = flag_out[0]
    to_smem.wait()
    src_copy.wait()

    for n in range(6):
        pack_send(n)
    spread_forward(0, rows_all)
    spread_start(1, w_out.at[0], w_all[0])
    spread_start(2, w_in.at[1], w_next)
    w_all[0][me_h] = w_out[0]
    w_all[1][me_h] = w_out[1]
    w_next[me_h] = w_in[1]
    spread_wait(0, rows_all)
    project_head()
    for n in range(6, 11):
        pack_send(n)
    spread_forward(1, w_all[0])
    pack_send(11)
    z_wait(0)
    attend(0, 0)
    attend(0, 1)
    pack_send(12)
    pack_send(13)
    spread_drain(0, rows_all)
    spread_forward(2, w_next)
    spread_start(3, w_out.at[1], w_all[1])
    spread_wait(1, w_all[0])
    wait_bytes(gate_recv[0].at[pl.ds(0, HEADS - 1)], cross_rsem.at[0])
    state[...] = finish(0).astype(BF16).astype(F32)
    pack_send(14)
    spread_wait(2, w_next)
    project_rows()
    pack_send(15)
    spread_forward(3, w_all[1])
    wait_bytes(req_in.at[pl.ds(0, NZ - 1)], req_ssem)
    wait_bytes(flag_in.at[pl.ds(0, NY - 1)], flag_rsem)
    wait_bytes(flag_in.at[pl.ds(0, NY - 1)], flag_ssem)
    flag_all[...] = jnp.max(flag_in[...], axis=0)
    to_smem = pltpu.make_async_copy(flag_all, flag_smem, smem_sem.at[0])
    to_smem.start()
    to_smem.wait()
    overflow[0] = flag_smem[0, 127]
    wait_bytes(q_buf[1].at[pl.ds(0, HEADS - 1)], cross_rsem.at[1])
    spread_wait(3, w_all[1])
    spread_drain(1, w_all[0])
    spread_drain(2, w_next)
    spread_drain(3, w_all[1])
    for layer in range(LAYERS):
        wait_bytes(out_send.at[layer, pl.ds(0, HEADS - 1)], cross_ssem.at[layer])
        wait_bytes(arr[layer].at[pl.ds(0, NZ * (NY - 1) * 2)], y_ssem.at[layer])
    wait_bytes(pack[0], z_ssem.at[0])
    wait_bytes(att_send[0].at[pl.ds(0, HEADS - 1)], att_ssem.at[0])
    z_wait(1)
    attend(1, 0)
    attend(1, 1)
    out[...] = finish(1).astype(BF16)
    wait_bytes(pack[1], z_ssem.at[1])
    wait_bytes(att_send[1].at[pl.ds(0, HEADS - 1)], att_ssem.at[1])


def both(shape, dtype=BF16):
    return [pltpu.VMEM(shape, dtype)] * LAYERS


def run(turn, lengths, owners, cand, w_in, w_out, pool):
    C = CAPS[turn]
    dma = pltpu.SemaphoreType.DMA
    vmem = pl.BlockSpec(memory_space=pltpu.VMEM)
    smem = pl.BlockSpec(memory_space=pltpu.SMEM)
    return pl.pallas_call(
        functools.partial(kernel, C),
        out_shape=(
            jax.ShapeDtypeStruct((BLOCK, D), BF16),
            jax.ShapeDtypeStruct((1,), jnp.int32),
        ),
        in_specs=[
            smem,
            smem,
            vmem,
            vmem,
            vmem,
            pl.BlockSpec(memory_space=pl.ANY),
        ],
        out_specs=(vmem, smem),
        scratch_shapes=[
            *both((NZ * C + 1, PAGE, 2 * DH)),
            *both((NZ - 1, C, PAGE, 2 * DH)),
            *both((HEADS, DH, D)),
            *both((HEADS, BLOCK, DH)),
            *both((HEADS, BLOCK, DH)),
            *both((HEADS, BLOCK, DH)),
            *both((HEADS, BLOCK, DH)),
            *[pltpu.VMEM((2 * NY, PAGE, 2 * DH), BF16)] * (LAYERS * NZ),
            pltpu.VMEM((HEADS, BLOCK, D), BF16),
            pltpu.VMEM((HEADS, D, 4 * DH), BF16),
            pltpu.VMEM((HEADS, BLOCK, DH), BF16),
            pltpu.VMEM((HEADS, BLOCK, DH), BF16),
            pltpu.VMEM((HEADS, BLOCK, DH), F32),
            pltpu.VMEM((LAYERS, HEADS, BLOCK, DH), BF16),
            pltpu.VMEM((PAGES * PAGE, DH), BF16),
            pltpu.VMEM((PAGES * PAGE, DH), BF16),
            pltpu.VMEM((BLOCK, D), F32),
            pltpu.VMEM((NZ, 1, 128), jnp.int32),
            pltpu.VMEM((NZ, 1, 128), jnp.int32),
            pltpu.SMEM((NZ, 1, 128), jnp.int32),
            pltpu.VMEM((USERS * PAGES, 128), jnp.int32),
            pltpu.SMEM((USERS * PAGES, 128), jnp.int32),
            pltpu.VMEM((1, 1, 128), jnp.int32),
            pltpu.VMEM((NY, 1, 128), jnp.int32),
            pltpu.VMEM((1, 128), jnp.int32),
            pltpu.SMEM((1, 128), jnp.int32),
            dma((LAYERS,)),
            dma((LAYERS * NZ,)),
            dma((LAYERS,)),
            dma((LAYERS,)),
            dma,
            dma,
            dma,
            dma,
            dma((2,)),
            dma((4,)),
            dma((4, HEADS)),
            dma((LAYERS,)),
            dma((LAYERS,)),
            dma((LAYERS,)),
            dma((LAYERS,)),
        ],
        compiler_params=pltpu.CompilerParams(
            collective_id=turn, has_side_effects=True, vmem_limit_bytes=62 * 2**20
        ),
    )(lengths, owners, cand, w_in, w_out, pool)


def shards(candidates, proj_in, proj_out, page_pool, page_owner, history_pages):
    owners = page_owner.transpose(0, 2, 1)
    args = (history_pages, owners, candidates, proj_in, proj_out, page_pool[0])
    first, overflow = run(0, *args)
    return lax.switch(overflow[0], [lambda: first, lambda: run(1, *args)[0]])


def solution(mesh):
    return jax.shard_map(
        shards,
        mesh=mesh,
        in_specs=(
            P(("cache", "head"), None),
            P(None, None, "head"),
            P(None, "head", None),
            P("cache", None, None, None, None, "head"),
            P("cache", None, None),
            P("cache"),
        ),
        out_specs=P(("cache", "head"), None),
        check_vma=False,
    )
```

```python
import functools

import jax
import jax.numpy as jnp
from jax import lax
from jax.experimental import pallas as pl
from jax.experimental.pallas import tpu as pltpu
from jax.sharding import PartitionSpec as P

MESH = pl.DeviceIdType.MESH
DH = 128
D = 1024
PAGE = 128
LAYERS = 2
USERS = 2
PAGES = 16
NY = 4
NZ = 8
NX = 4
HEADS = 8
BLOCK = 256
MOST = 2 * NY
CAPS = (5, 6, MOST)
WINDOW = 3
OFFSETS = (4, 3, 5, 2, 6, 1, 7, 0)
F32 = jnp.float32
BF16 = jnp.bfloat16


def half_silu(t):
    return t * jnp.tanh(t) + t


def remote(src_ref, dst_ref, send, recv, cache, head):
    return pltpu.make_async_remote_copy(
        src_ref=src_ref,
        dst_ref=dst_ref,
        send_sem=send,
        recv_sem=recv,
        device_id=(cache, head),
        device_id_type=MESH,
    )


def wait_bytes(ref, sem):
    pltpu.make_async_copy(ref, ref, sem).wait()


def place_of_device():
    me_c = lax.axis_index("cache")
    my_y = me_c // NZ
    my_z = lax.rem(me_c, NZ)

    def y_peer(dy):
        return lax.rem(my_y + dy, NY)

    def z_peer(dz):
        return lax.rem(my_z + dz, NZ)

    return me_c, lax.axis_index("head"), my_y, my_z, y_peer, z_peer


def greet(devices):
    barrier = pltpu.get_barrier_semaphore()
    for device in devices:
        pl.semaphore_signal(barrier, inc=1, device_id=device, device_id_type=MESH)
    return lambda: pl.semaphore_wait(barrier, len(devices))


def y_copies(pool, target, n, send, recv):
    me_c, me_h, my_y, my_z, y_peer, z_peer = place_of_device()
    layer, i = divmod(n, NZ)
    column = z_peer(OFFSETS[i])
    place = target.at[pl.ds(my_y * 2, 2)]
    for dy in (2, 1, 3):
        remote(
            pool.at[y_peer(dy) * NZ + column, :, layer],
            place,
            send,
            recv,
            y_peer(dy) * NZ + my_z,
            me_h,
        ).start()
    pltpu.make_async_copy(pool.at[my_y * NZ + column, :, layer], place, recv).start()


def request_kernel(
    lengths,
    owners,
    pool,
    src,
    req_in,
    y_first,
    level,
    req_out,
    flag_out,
    flag_in,
    flag_all,
    flag_smem,
    y_ssem,
    y_rsem,
    req_ssem,
    req_rsem,
    flag_ssem,
    flag_rsem,
    smem_sem,
):
    me_c, me_h, my_y, my_z, y_peer, z_peer = place_of_device()
    greeted = greet(
        [(y_peer(dy) * NZ + my_z, me_h) for dy in range(1, NY)]
        + [(my_y * NZ + z_peer(dz), me_h) for dz in range(1, NZ)]
    )
    count = USERS * PAGES
    lane = lax.broadcasted_iota(jnp.int32, (count, count), 1)
    sub = lax.broadcasted_iota(jnp.int32, (count, count), 0)
    row = jnp.zeros((1, count), jnp.int32)
    col = jnp.zeros((count, 1), jnp.int32)
    for p in range(count):
        owner = owners[p // PAGES, 0, p % PAGES]
        row = jnp.where(lane[:1] == p, owner, row)
        col = jnp.where(sub[:, :1] == p, owner, col)

    def live_of(index):
        length = jnp.where(index < PAGES, lengths[0], lengths[1])
        return lax.rem(index, PAGES) < length

    def total(mask, axis):
        return jnp.sum(mask.astype(jnp.int32), axis=axis, keepdims=True)

    slot = jnp.minimum(total((row == col) & (lane < sub), 1), 1)
    same = lax.rem(row, NZ) == lax.rem(col, NZ)
    rank = total(same & (lane < sub) & live_of(lane), 1)
    live = live_of(sub[:, :1])
    place = lax.rem(col // NZ, NY) * 2 + slot
    target = jnp.where(live, lax.rem(col, NZ) * MOST + rank, NZ * MOST)
    need = jnp.max(jnp.where(live, rank + 1, 0), axis=0, keepdims=True)
    rank_row = total(same & (sub < lane) & live_of(sub), 0)
    target_row = jnp.where(live_of(lane[:1]), lax.rem(row, NZ) * MOST + rank_row, NZ * MOST)
    src[...] = jnp.zeros_like(src)
    src[:, 0:count] = target_row
    lanes = lax.broadcasted_iota(jnp.int32, (count, 128), 1)
    for z in range(NZ):
        hit = (target == lanes + z * MOST) & (lanes < MOST)
        line = jnp.sum(jnp.where(hit, place, 0), axis=0, keepdims=True)
        req_out[z] = jnp.where(lanes[:1] == 127, need, line)

    greeted()
    for dz in range(1, NZ):
        column = z_peer(dz)
        remote(
            req_out.at[column],
            req_in.at[my_z],
            req_ssem,
            req_rsem,
            my_y * NZ + column,
            me_h,
        ).start()
    y_copies(pool, y_first, 0, y_ssem, y_rsem)
    req_in[my_z] = req_out[my_z]
    wait_bytes(req_out.at[pl.ds(0, NZ - 1)], req_rsem)
    flag_out[0] = jnp.max(req_in[...], axis=0)
    for dy in range(1, NY):
        remote(
            flag_out.at[0],
            flag_in.at[my_y],
            flag_ssem,
            flag_rsem,
            y_peer(dy) * NZ + my_z,
            me_h,
        ).start()
    flag_in[my_y] = flag_out[0]
    wait_bytes(req_out.at[pl.ds(0, NY - 1)], flag_rsem)
    most = jnp.max(flag_in[...], axis=0)
    flag_all[...] = (most > CAPS[0]).astype(jnp.int32) + (most > CAPS[1]).astype(jnp.int32)
    to_smem = pltpu.make_async_copy(flag_all, flag_smem, smem_sem)
    to_smem.start()
    to_smem.wait()
    level[0] = flag_smem[0, 127]
    wait_bytes(req_out.at[pl.ds(0, NZ - 1)], req_ssem)
    wait_bytes(req_out.at[pl.ds(0, NY - 1)], flag_ssem)
    wait_bytes(y_first.at[pl.ds(0, 2 * (NY - 1))], y_ssem)
    wait_bytes(y_first, y_rsem)


def kernel(
    C,
    lengths,
    src,
    req,
    cand,
    w_in,
    w_out,
    y_first,
    pool,
    out,
    *scratch,
):
    (
        arr,
        pack,
        w_all,
        gate_recv,
        q_buf,
        att_send,
        att_recv,
    ) = [scratch[2 * i : 2 * i + 2] for i in range(7)]
    ybuf = (y_first, *scratch[14:29])
    (
        rows_all,
        w_next,
        k_buf,
        v_buf,
        own_buf,
        out_send,
        keys,
        values,
        state,
        y_ssem,
        y_rsem,
        z_ssem,
        z_rsem,
        spread_ssem,
        spread_rsem,
        cross_ssem,
        cross_rsem,
        att_ssem,
        att_rsem,
    ) = scratch[29:]

    ZERO = NZ * C
    me_c, me_h, my_y, my_z, y_peer, z_peer = place_of_device()
    my_x = me_h // 2
    core = lax.rem(me_h, 2)
    sibling = my_x * 2 + (1 - core)

    def head_peer(dx, dcore):
        return lax.rem(my_x + dx, NX) * 2 + lax.rem(core + dcore, 2)

    head_steps = [(dx, dc) for dx in range(NX) for dc in range(2) if (dx, dc) != (0, 0)]
    greeted = greet(
        [(y_peer(dy) * NZ + my_z, me_h) for dy in range(1, NY)]
        + [(my_y * NZ + z_peer(dz), me_h) for dz in range(1, NZ)]
        + [(me_c, head_peer(dx, dc)) for dx, dc in head_steps]
    )

    def y_start(n):
        y_copies(pool, ybuf[n], n, y_ssem.at[n], y_rsem.at[n])

    def pack_send(n):
        if n + WINDOW < LAYERS * NZ:
            y_start(n + WINDOW)
        layer, i = divmod(n, NZ)
        if n > 0:
            wait_bytes(ybuf[n], y_rsem.at[n])
        column = z_peer(OFFSETS[i])
        for j in range(C):
            page = ybuf[n][jnp.clip(req[column, 0, j], 0, MOST - 1)]
            if OFFSETS[i] == 0:
                arr[layer][my_z * C + j] = page
            else:
                pack[layer][i, j] = page
        if OFFSETS[i] != 0:
            remote(
                pack[layer].at[i],
                arr[layer].at[pl.ds(my_z * C, C)],
                z_ssem.at[layer],
                z_rsem.at[layer],
                my_y * NZ + column,
                me_h,
            ).start()

    def z_wait(layer):
        wait_bytes(arr[layer].at[pl.ds(0, (NZ - 1) * C)], z_rsem.at[layer])

    def spread_start(k, block, places):
        for dx in (2, 1, 3):
            remote(
                block,
                places.at[me_h],
                spread_ssem.at[k],
                spread_rsem.at[k, me_h],
                me_c,
                head_peer(dx, 0),
            ).start()
        remote(
            block, places.at[me_h], spread_ssem.at[k], spread_rsem.at[k, me_h], me_c, sibling
        ).start()

    def spread_forward(k, places):
        for dx in (1, 3, 2):
            source = head_peer(dx, 0)
            place = places.at[source]
            wait_bytes(place, spread_rsem.at[k, source])
            remote(
                place, place, spread_ssem.at[k], spread_rsem.at[k, source], me_c, sibling
            ).start()

    def spread_wait(k, places):
        for dx in (0, 1, 3, 2):
            source = head_peer(dx, 1)
            wait_bytes(places.at[source], spread_rsem.at[k, source])

    def spread_drain(k, places):
        wait_bytes(places.at[pl.ds(0, HEADS - 1)], spread_ssem.at[k])

    def normed_rows():
        xf = state[...]
        normed = xf * lax.rsqrt(jnp.mean(xf * xf, axis=-1, keepdims=True) + 1e-06)
        return normed.astype(BF16)

    def activations(rows, w):
        act = jnp.dot(rows, w, preferred_element_type=F32)
        act = half_silu(act * 0.5).astype(BF16)
        return [act[:, i * DH : (i + 1) * DH] for i in range(4)]

    def reciprocal(user):
        return 1.0 / jnp.full((1, DH), lengths[user] * PAGE + 1, jnp.int32).astype(F32)

    def own_term(query, key, value):
        own = jnp.sum(query.astype(F32) * key.astype(F32), axis=-1, keepdims=True)
        return half_silu(own * (0.5 * DH**-0.5)) * value.astype(F32)

    def project_head():
        def body(i, carry):
            gate, value, query, key = activations(rows_all[i], w_in[0])
            out_send[0, i] = gate
            v_buf[i] = value
            q_buf[0][i] = query
            k_buf[i] = key
            return carry

        lax.fori_loop(0, HEADS, body, 0)
        for dx, dc in head_steps:
            cross_copy(0, head_peer(dx, dc)).start()
        gate_recv[0][me_h] = out_send[0, me_h]

    def cross_copy(layer, peer):
        return remote(
            out_send.at[layer, peer],
            (gate_recv[0] if layer == 0 else q_buf[1]).at[me_h],
            cross_ssem.at[layer],
            cross_rsem.at[layer],
            me_c,
            peer,
        )

    def project_rows():
        rows_all[0] = normed_rows()
        scale = reciprocal(me_h // (HEADS // USERS))

        def one(head):
            gate, value, query, key = activations(rows_all[0], w_next[head])
            gate_recv[1][head] = gate
            own_buf[head] = own_term(query, key, value) * scale
            return query

        def body(step, carry):
            head = lax.rem(me_h + step, HEADS)
            out_send[1, head] = one(head)
            cross_copy(1, head).start()
            return carry

        lax.fori_loop(1, HEADS, body, 0)
        q_buf[1][me_h] = one(me_h)

    def att_copy(layer, peer):
        return remote(
            att_send[layer].at[peer],
            att_recv[layer].at[me_h],
            att_ssem.at[layer],
            att_rsem.at[layer],
            me_c,
            peer,
        )

    def attend(layer):
        per_user = HEADS // USERS

        def body(user, carry):
            for p in range(PAGES):
                target = src[0, user * PAGES + p]
                page = arr[layer][
                    jnp.clip((target // MOST) * C + lax.rem(target, MOST), 0, ZERO)
                ]
                keys[pl.ds(p * PAGE, PAGE)] = page[:, :DH]
                values[pl.ds(p * PAGE, PAGE)] = page[:, DH:]
            query = q_buf[layer][pl.ds(user * per_user, per_user)]
            query = query.reshape(per_user * BLOCK, DH)
            total = jnp.zeros((per_user * BLOCK, DH), F32)
            for e in range(0, PAGES * PAGE, 2 * PAGE):
                score = lax.dot_general(
                    query,
                    keys[pl.ds(e, 2 * PAGE)],
                    (((1,), (1,)), ((), ())),
                    preferred_element_type=F32,
                )
                weights = half_silu(score * (0.5 * DH**-0.5)).astype(BF16)
                total = total + jnp.dot(
                    weights, values[pl.ds(e, 2 * PAGE)], preferred_element_type=F32
                )
            scale = reciprocal(user)
            for r in range(per_user):
                block = user * per_user + r
                here = total[r * BLOCK : (r + 1) * BLOCK]
                if layer == 0:
                    here = here + own_term(q_buf[0][block], k_buf[block], v_buf[block])
                att_send[layer][block] = (here * scale).astype(BF16)
            for r in range(per_user):
                block = user * per_user + r

                @pl.when(block != me_h)
                def _():
                    att_copy(layer, block).start()

                @pl.when(block == me_h)
                def _():
                    att_recv[layer][block] = att_send[layer][block]

            return carry

        lax.fori_loop(0, USERS, body, 0)

    def finish(layer):
        wait_bytes(att_recv[layer].at[pl.ds(0, HEADS - 1)], att_rsem.at[layer])
        att = [att_recv[layer][h].astype(F32) for h in range(HEADS)]
        if layer == 1:
            att = [att[h] + own_buf[h] for h in range(HEADS)]
        first = sum([jnp.sum(a, axis=-1, keepdims=True) for a in att]) * (1.0 / D)
        second = sum([jnp.sum(a * a, axis=-1, keepdims=True) for a in att]) * (1.0 / D)
        rstd = lax.rsqrt(second - first * first + 1e-05)
        update = state[...]
        for h in range(0, HEADS, 2):
            pair = [
                ((att[i] - first) * rstd * gate_recv[layer][i].astype(F32)).astype(BF16)
                for i in (h, h + 1)
            ]
            w_pair = jnp.concatenate([w_all[layer][h], w_all[layer][h + 1]], axis=0)
            update = update + jnp.dot(
                jnp.concatenate(pair, axis=1), w_pair, preferred_element_type=F32
            )
        return update

    state[...] = cand[...].astype(F32)
    rows_all[me_h] = normed_rows()
    for layer in range(LAYERS):
        arr[layer][ZERO] = jnp.zeros((PAGE, 2 * DH), BF16)
    greeted()
    for n in range(1, WINDOW):
        y_start(n)
    pack_send(0)
    spread_start(0, rows_all.at[me_h], rows_all)
    for n in range(1, 6):
        pack_send(n)
    spread_forward(0, rows_all)
    spread_start(1, w_out.at[0], w_all[0])
    spread_start(2, w_in.at[1], w_next)
    w_all[0][me_h] = w_out[0]
    w_all[1][me_h] = w_out[1]
    w_next[me_h] = w_in[1]
    spread_wait(0, rows_all)
    project_head()
    for n in range(6, 11):
        pack_send(n)
    spread_forward(1, w_all[0])
    pack_send(11)
    z_wait(0)
    attend(0)
    pack_send(12)
    pack_send(13)
    spread_drain(0, rows_all)
    spread_forward(2, w_next)
    spread_start(3, w_out.at[1], w_all[1])
    spread_wait(1, w_all[0])
    wait_bytes(gate_recv[0].at[pl.ds(0, HEADS - 1)], cross_rsem.at[0])
    state[...] = finish(0).astype(BF16).astype(F32)
    pack_send(14)
    spread_wait(2, w_next)
    project_rows()
    pack_send(15)
    spread_forward(3, w_all[1])
    wait_bytes(q_buf[1].at[pl.ds(0, HEADS - 1)], cross_rsem.at[1])
    spread_wait(3, w_all[1])
    spread_drain(1, w_all[0])
    spread_drain(2, w_next)
    spread_drain(3, w_all[1])
    for layer in range(LAYERS):
        wait_bytes(out_send.at[layer, pl.ds(0, HEADS - 1)], cross_ssem.at[layer])
    for n in range(1, LAYERS * NZ):
        wait_bytes(ybuf[n].at[pl.ds(0, 2 * (NY - 1))], y_ssem.at[n])
    wait_bytes(pack[0], z_ssem.at[0])
    wait_bytes(att_send[0].at[pl.ds(0, HEADS - 1)], att_ssem.at[0])
    z_wait(1)
    attend(1)
    out[...] = finish(1).astype(BF16)
    wait_bytes(pack[1], z_ssem.at[1])
    wait_bytes(att_send[1].at[pl.ds(0, HEADS - 1)], att_ssem.at[1])


def both(shape, dtype=BF16):
    return [pltpu.VMEM(shape, dtype)] * LAYERS


def ask(lengths, owners, pool):
    dma = pltpu.SemaphoreType.DMA
    vmem = pl.BlockSpec(memory_space=pltpu.VMEM)
    smem = pl.BlockSpec(memory_space=pltpu.SMEM)
    return pl.pallas_call(
        request_kernel,
        out_shape=(
            jax.ShapeDtypeStruct((1, 128), jnp.int32),
            jax.ShapeDtypeStruct((NZ, 1, 128), jnp.int32),
            jax.ShapeDtypeStruct((2 * NY, PAGE, 2 * DH), BF16),
            jax.ShapeDtypeStruct((1,), jnp.int32),
        ),
        in_specs=[smem, smem, pl.BlockSpec(memory_space=pl.ANY)],
        out_specs=(vmem, vmem, vmem, smem),
        scratch_shapes=[
            pltpu.VMEM((NZ, 1, 128), jnp.int32),
            pltpu.VMEM((1, 1, 128), jnp.int32),
            pltpu.VMEM((NY, 1, 128), jnp.int32),
            pltpu.VMEM((1, 128), jnp.int32),
            pltpu.SMEM((1, 128), jnp.int32),
            *[dma] * 7,
        ],
        compiler_params=pltpu.CompilerParams(collective_id=0, has_side_effects=True),
    )(lengths, owners, pool)


def run(turn, *args):
    C = CAPS[turn]
    dma = pltpu.SemaphoreType.DMA
    vmem = pl.BlockSpec(memory_space=pltpu.VMEM)
    smem = pl.BlockSpec(memory_space=pltpu.SMEM)
    return pl.pallas_call(
        functools.partial(kernel, C),
        out_shape=jax.ShapeDtypeStruct((BLOCK, D), BF16),
        in_specs=[
            smem,
            smem,
            smem,
            vmem,
            vmem,
            vmem,
            vmem,
            pl.BlockSpec(memory_space=pl.ANY),
        ],
        out_specs=vmem,
        scratch_shapes=[
            *both((NZ * C + 1, PAGE, 2 * DH)),
            *both((NZ - 1, C, PAGE, 2 * DH)),
            *both((HEADS, DH, D)),
            *both((HEADS, BLOCK, DH)),
            *both((HEADS, BLOCK, DH)),
            *both((HEADS, BLOCK, DH)),
            *both((HEADS, BLOCK, DH)),
            *[pltpu.VMEM((2 * NY, PAGE, 2 * DH), BF16)] * (LAYERS * NZ - 1),
            pltpu.VMEM((HEADS, BLOCK, D), BF16),
            pltpu.VMEM((HEADS, D, 4 * DH), BF16),
            pltpu.VMEM((HEADS, BLOCK, DH), BF16),
            pltpu.VMEM((HEADS, BLOCK, DH), BF16),
            pltpu.VMEM((HEADS, BLOCK, DH), F32),
            pltpu.VMEM((LAYERS, HEADS, BLOCK, DH), BF16),
            pltpu.VMEM((PAGES * PAGE, DH), BF16),
            pltpu.VMEM((PAGES * PAGE, DH), BF16),
            pltpu.VMEM((BLOCK, D), F32),
            dma((LAYERS * NZ,)),
            dma((LAYERS * NZ,)),
            dma((LAYERS,)),
            dma((LAYERS,)),
            dma((4,)),
            dma((4, HEADS)),
            dma((LAYERS,)),
            dma((LAYERS,)),
            dma((LAYERS,)),
            dma((LAYERS,)),
        ],
        compiler_params=pltpu.CompilerParams(
            collective_id=turn + 1, has_side_effects=True, vmem_limit_bytes=62 * 2**20
        ),
    )(*args)


def shards(candidates, proj_in, proj_out, page_pool, page_owner, history_pages):
    pool = page_pool[0]
    src, req, y_first, level = ask(history_pages, page_owner.transpose(0, 2, 1), pool)
    args = (history_pages, src, req, candidates, proj_in, proj_out, y_first, pool)
    return lax.switch(level[0], [functools.partial(run, turn, *args) for turn in range(len(CAPS))])


def solution(mesh):
    return jax.shard_map(
        shards,
        mesh=mesh,
        in_specs=(
            P(("cache", "head"), None),
            P(None, None, "head"),
            P(None, "head", None),
            P("cache", None, None, None, None, "head"),
            P("cache", None, None),
            P("cache"),
        ),
        out_specs=P(("cache", "head"), None),
        check_vma=False,
    )
```

```python
import functools

import jax
import jax.numpy as jnp
from jax import lax
from jax.experimental import pallas as pl
from jax.experimental.pallas import tpu as pltpu
from jax.sharding import PartitionSpec as P

MESH = pl.DeviceIdType.MESH
DH = 128
D = 1024
PAGE = 128
LAYERS = 2
USERS = 2
PAGES = 16
NY = 4
NZ = 8
NX = 4
HEADS = 8
BLOCK = 256
MOST = 2 * NY
CAPS = (5, 6, MOST)
WINDOW = 3
OFFSETS = (4, 3, 5, 2, 6, 1, 7, 0)
F32 = jnp.float32
BF16 = jnp.bfloat16


def half_silu(t):
    return t * jnp.tanh(t) + t


def remote(src_ref, dst_ref, send, recv, cache, head):
    return pltpu.make_async_remote_copy(
        src_ref=src_ref,
        dst_ref=dst_ref,
        send_sem=send,
        recv_sem=recv,
        device_id=(cache, head),
        device_id_type=MESH,
    )


def wait_bytes(ref, sem):
    pltpu.make_async_copy(ref, ref, sem).wait()


def place_of_device():
    me_c = lax.axis_index("cache")
    my_y = me_c // NZ
    my_z = lax.rem(me_c, NZ)

    def y_peer(dy):
        return lax.rem(my_y + dy, NY)

    def z_peer(dz):
        return lax.rem(my_z + dz, NZ)

    return me_c, lax.axis_index("head"), my_y, my_z, y_peer, z_peer


def greet(devices):
    barrier = pltpu.get_barrier_semaphore()
    for device in devices:
        pl.semaphore_signal(barrier, inc=1, device_id=device, device_id_type=MESH)
    return lambda: pl.semaphore_wait(barrier, len(devices))


def y_copies(pool, target, n, send, recv):
    me_c, me_h, my_y, my_z, y_peer, z_peer = place_of_device()
    layer, i = divmod(n, NZ)
    column = z_peer(OFFSETS[i])
    place = target.at[pl.ds(my_y * 2, 2)]
    for dy in (2, 1, 3):
        remote(
            pool.at[y_peer(dy) * NZ + column, :, layer],
            place,
            send,
            recv,
            y_peer(dy) * NZ + my_z,
            me_h,
        ).start()
    pltpu.make_async_copy(pool.at[my_y * NZ + column, :, layer], place, recv).start()


def request_kernel(
    lengths,
    owners,
    pool,
    src,
    req_in,
    y_first,
    level,
    req_out,
    flag_out,
    flag_in,
    flag_all,
    flag_smem,
    y_ssem,
    y_rsem,
    req_ssem,
    req_rsem,
    flag_ssem,
    flag_rsem,
    smem_sem,
):
    me_c, me_h, my_y, my_z, y_peer, z_peer = place_of_device()
    greeted = greet(
        [(y_peer(dy) * NZ + my_z, me_h) for dy in range(1, NY)]
        + [(my_y * NZ + z_peer(dz), me_h) for dz in range(1, NZ)]
    )
    count = USERS * PAGES
    lane = lax.broadcasted_iota(jnp.int32, (count, count), 1)
    sub = lax.broadcasted_iota(jnp.int32, (count, count), 0)
    row = jnp.zeros((1, count), jnp.int32)
    col = jnp.zeros((count, 1), jnp.int32)
    for p in range(count):
        owner = owners[p // PAGES, 0, p % PAGES]
        row = jnp.where(lane[:1] == p, owner, row)
        col = jnp.where(sub[:, :1] == p, owner, col)

    def live_of(index):
        length = jnp.where(index < PAGES, lengths[0], lengths[1])
        return lax.rem(index, PAGES) < length

    def total(mask, axis):
        return jnp.sum(mask.astype(jnp.int32), axis=axis, keepdims=True)

    slot = jnp.minimum(total((row == col) & (lane < sub), 1), 1)
    same = lax.rem(row, NZ) == lax.rem(col, NZ)
    rank = total(same & (lane < sub) & live_of(lane), 1)
    live = live_of(sub[:, :1])
    place = lax.rem(col // NZ, NY) * 2 + slot
    target = jnp.where(live, lax.rem(col, NZ) * MOST + rank, NZ * MOST)
    need = jnp.max(jnp.where(live, rank + 1, 0), axis=0, keepdims=True)
    rank_row = total(same & (sub < lane) & live_of(sub), 0)
    target_row = jnp.where(live_of(lane[:1]), lax.rem(row, NZ) * MOST + rank_row, NZ * MOST)
    src[...] = jnp.zeros_like(src)
    src[:, 0:count] = target_row
    lanes = lax.broadcasted_iota(jnp.int32, (count, 128), 1)
    for z in range(NZ):
        hit = (target == lanes + z * MOST) & (lanes < MOST)
        line = jnp.sum(jnp.where(hit, place, 0), axis=0, keepdims=True)
        req_out[z] = jnp.where(lanes[:1] == 127, need, line)

    greeted()
    for dz in range(1, NZ):
        column = z_peer(dz)
        remote(
            req_out.at[column],
            req_in.at[my_z],
            req_ssem,
            req_rsem,
            my_y * NZ + column,
            me_h,
        ).start()
    y_copies(pool, y_first, 0, y_ssem, y_rsem)
    req_in[my_z] = req_out[my_z]
    wait_bytes(req_out.at[pl.ds(0, NZ - 1)], req_rsem)
    flag_out[0] = jnp.max(req_in[...], axis=0)
    for dy in range(1, NY):
        remote(
            flag_out.at[0],
            flag_in.at[my_y],
            flag_ssem,
            flag_rsem,
            y_peer(dy) * NZ + my_z,
            me_h,
        ).start()
    flag_in[my_y] = flag_out[0]
    wait_bytes(req_out.at[pl.ds(0, NY - 1)], flag_rsem)
    most = jnp.max(flag_in[...], axis=0)
    flag_all[...] = (most > CAPS[0]).astype(jnp.int32) + (most > CAPS[1]).astype(jnp.int32)
    to_smem = pltpu.make_async_copy(flag_all, flag_smem, smem_sem)
    to_smem.start()
    to_smem.wait()
    level[0] = flag_smem[0, 127]
    wait_bytes(req_out.at[pl.ds(0, NZ - 1)], req_ssem)
    wait_bytes(req_out.at[pl.ds(0, NY - 1)], flag_ssem)
    wait_bytes(y_first.at[pl.ds(0, 2 * (NY - 1))], y_ssem)
    wait_bytes(y_first, y_rsem)


def kernel(
    C,
    lengths,
    src,
    req,
    cand,
    w_in,
    w_out,
    y_first,
    pool,
    out,
    *scratch,
):
    (
        arr,
        pack,
        w_all,
        gate_recv,
        q_buf,
        att_send,
        att_recv,
    ) = [scratch[2 * i : 2 * i + 2] for i in range(7)]
    ybuf = (y_first, *scratch[14:29])
    (
        rows_all,
        w_next,
        k_buf,
        v_buf,
        own_buf,
        out_send,
        keys,
        values,
        state,
        y_ssem,
        y_rsem,
        z_ssem,
        z_rsem,
        spread_ssem,
        spread_rsem,
        cross_ssem,
        cross_rsem,
        att_ssem,
        att_rsem,
    ) = scratch[29:]

    ZERO = NZ * C
    me_c, me_h, my_y, my_z, y_peer, z_peer = place_of_device()
    my_x = me_h // 2
    core = lax.rem(me_h, 2)
    sibling = my_x * 2 + (1 - core)

    def head_peer(dx, dcore):
        return lax.rem(my_x + dx, NX) * 2 + lax.rem(core + dcore, 2)

    head_steps = [(dx, dc) for dx in range(NX) for dc in range(2) if (dx, dc) != (0, 0)]
    greeted = greet(
        [(y_peer(dy) * NZ + my_z, me_h) for dy in range(1, NY)]
        + [(my_y * NZ + z_peer(dz), me_h) for dz in range(1, NZ)]
        + [(me_c, head_peer(dx, dc)) for dx, dc in head_steps]
    )

    def y_start(n):
        y_copies(pool, ybuf[n], n, y_ssem.at[n], y_rsem.at[n])

    def pack_send(n):
        if n + WINDOW < LAYERS * NZ:
            y_start(n + WINDOW)
        layer, i = divmod(n, NZ)
        if n > 0:
            wait_bytes(ybuf[n], y_rsem.at[n])
        column = z_peer(OFFSETS[i])
        for j in range(C):
            page = ybuf[n][jnp.clip(req[column, 0, j], 0, MOST - 1)]
            if OFFSETS[i] == 0:
                arr[layer][my_z * C + j] = page
            else:
                pack[layer][i, j] = page
        if OFFSETS[i] != 0:
            remote(
                pack[layer].at[i],
                arr[layer].at[pl.ds(my_z * C, C)],
                z_ssem.at[layer],
                z_rsem.at[layer],
                my_y * NZ + column,
                me_h,
            ).start()

    def z_wait(layer):
        wait_bytes(arr[layer].at[pl.ds(0, (NZ - 1) * C)], z_rsem.at[layer])

    def spread_start(k, block, places):
        for dx in (2, 1, 3):
            remote(
                block,
                places.at[me_h],
                spread_ssem.at[k],
                spread_rsem.at[k, me_h],
                me_c,
                head_peer(dx, 0),
            ).start()
        remote(
            block, places.at[me_h], spread_ssem.at[k], spread_rsem.at[k, me_h], me_c, sibling
        ).start()

    def spread_forward(k, places):
        for dx in (1, 3, 2):
            source = head_peer(dx, 0)
            place = places.at[source]
            wait_bytes(place, spread_rsem.at[k, source])
            remote(
                place, place, spread_ssem.at[k], spread_rsem.at[k, source], me_c, sibling
            ).start()

    def spread_wait(k, places):
        for dx in (0, 1, 3, 2):
            source = head_peer(dx, 1)
            wait_bytes(places.at[source], spread_rsem.at[k, source])

    def spread_drain(k, places):
        wait_bytes(places.at[pl.ds(0, HEADS - 1)], spread_ssem.at[k])

    def normed_rows():
        xf = state[...]
        normed = xf * lax.rsqrt(jnp.mean(xf * xf, axis=-1, keepdims=True) + 1e-06)
        return normed.astype(BF16)

    def activations(rows, w):
        act = jnp.dot(rows, w, preferred_element_type=F32)
        act = half_silu(act * 0.5).astype(BF16)
        return [act[:, i * DH : (i + 1) * DH] for i in range(4)]

    def reciprocal(user):
        return 1.0 / jnp.full((1, DH), lengths[user] * PAGE + 1, jnp.int32).astype(F32)

    def own_term(query, key, value):
        own = jnp.sum(query.astype(F32) * key.astype(F32), axis=-1, keepdims=True)
        return half_silu(own * (0.5 * DH**-0.5)) * value.astype(F32)

    def project_head():
        def body(i, carry):
            gate, value, query, key = activations(rows_all[i], w_in[0])
            out_send[0, i] = gate
            v_buf[i] = value
            q_buf[0][i] = query
            k_buf[i] = key
            return carry

        lax.fori_loop(0, HEADS, body, 0)
        for dx, dc in head_steps:
            cross_copy(0, head_peer(dx, dc)).start()
        gate_recv[0][me_h] = out_send[0, me_h]

    def cross_copy(layer, peer):
        return remote(
            out_send.at[layer, peer],
            (gate_recv[0] if layer == 0 else q_buf[1]).at[me_h],
            cross_ssem.at[layer],
            cross_rsem.at[layer],
            me_c,
            peer,
        )

    def project_rows():
        rows_all[0] = normed_rows()
        scale = reciprocal(me_h // (HEADS // USERS))

        def one(head):
            gate, value, query, key = activations(rows_all[0], w_next[head])
            gate_recv[1][head] = gate
            own_buf[head] = own_term(query, key, value) * scale
            return query

        def body(step, carry):
            head = lax.rem(me_h + step, HEADS)
            out_send[1, head] = one(head)
            cross_copy(1, head).start()
            return carry

        lax.fori_loop(1, HEADS, body, 0)
        q_buf[1][me_h] = one(me_h)

    def att_copy(layer, peer):
        return remote(
            att_send[layer].at[peer],
            att_recv[layer].at[me_h],
            att_ssem.at[layer],
            att_rsem.at[layer],
            me_c,
            peer,
        )

    def attend(layer):
        per_user = HEADS // USERS

        def body(user, carry):
            for p in range(PAGES):
                target = src[0, user * PAGES + p]
                page = arr[layer][
                    jnp.clip((target // MOST) * C + lax.rem(target, MOST), 0, ZERO)
                ]
                keys[pl.ds(p * PAGE, PAGE)] = page[:, :DH]
                values[pl.ds(p * PAGE, PAGE)] = page[:, DH:]
            query = q_buf[layer][pl.ds(user * per_user, per_user)]
            query = query.reshape(per_user * BLOCK, DH)
            total = jnp.zeros((per_user * BLOCK, DH), F32)
            for e in range(0, PAGES * PAGE, 2 * PAGE):
                score = lax.dot_general(
                    query,
                    keys[pl.ds(e, 2 * PAGE)],
                    (((1,), (1,)), ((), ())),
                    preferred_element_type=F32,
                )
                weights = half_silu(score * (0.5 * DH**-0.5)).astype(BF16)
                total = total + jnp.dot(
                    weights, values[pl.ds(e, 2 * PAGE)], preferred_element_type=F32
                )
            scale = reciprocal(user)
            for r in range(per_user):
                block = user * per_user + r
                here = total[r * BLOCK : (r + 1) * BLOCK]
                if layer == 0:
                    here = here + own_term(q_buf[0][block], k_buf[block], v_buf[block])
                att_send[layer][block] = (here * scale).astype(BF16)
            for r in range(per_user):
                block = user * per_user + r

                @pl.when(block != me_h)
                def _():
                    att_copy(layer, block).start()

                @pl.when(block == me_h)
                def _():
                    att_recv[layer][block] = att_send[layer][block]

            return carry

        lax.fori_loop(0, USERS, body, 0)

    def finish(layer):
        wait_bytes(att_recv[layer].at[pl.ds(0, HEADS - 1)], att_rsem.at[layer])
        att = [att_recv[layer][h].astype(F32) for h in range(HEADS)]
        if layer == 1:
            att = [att[h] + own_buf[h] for h in range(HEADS)]
        first = sum([jnp.sum(a, axis=-1, keepdims=True) for a in att]) * (1.0 / D)
        second = sum([jnp.sum(a * a, axis=-1, keepdims=True) for a in att]) * (1.0 / D)
        rstd = lax.rsqrt(second - first * first + 1e-05)
        update = state[...]
        for h in range(0, HEADS, 2):
            pair = [
                ((att[i] - first) * rstd * gate_recv[layer][i].astype(F32)).astype(BF16)
                for i in (h, h + 1)
            ]
            w_pair = jnp.concatenate([w_all[layer][h], w_all[layer][h + 1]], axis=0)
            update = update + jnp.dot(
                jnp.concatenate(pair, axis=1), w_pair, preferred_element_type=F32
            )
        return update

    state[...] = cand[...].astype(F32)
    rows_all[me_h] = normed_rows()
    for layer in range(LAYERS):
        arr[layer][ZERO] = jnp.zeros((PAGE, 2 * DH), BF16)
    greeted()
    for n in range(1, WINDOW):
        y_start(n)
    pack_send(0)
    spread_start(0, rows_all.at[me_h], rows_all)
    spread_start(1, w_out.at[0], w_all[0])
    spread_start(2, w_in.at[1], w_next)
    for n in range(1, 6):
        pack_send(n)
    spread_forward(0, rows_all)
    w_all[0][me_h] = w_out[0]
    w_all[1][me_h] = w_out[1]
    w_next[me_h] = w_in[1]
    spread_wait(0, rows_all)
    project_head()
    for n in range(6, 11):
        pack_send(n)
    spread_forward(1, w_all[0])
    pack_send(11)
    z_wait(0)
    attend(0)
    pack_send(12)
    pack_send(13)
    spread_drain(0, rows_all)
    spread_forward(2, w_next)
    spread_start(3, w_out.at[1], w_all[1])
    spread_wait(1, w_all[0])
    wait_bytes(gate_recv[0].at[pl.ds(0, HEADS - 1)], cross_rsem.at[0])
    state[...] = finish(0).astype(BF16).astype(F32)
    pack_send(14)
    spread_wait(2, w_next)
    project_rows()
    pack_send(15)
    spread_forward(3, w_all[1])
    wait_bytes(q_buf[1].at[pl.ds(0, HEADS - 1)], cross_rsem.at[1])
    spread_wait(3, w_all[1])
    spread_drain(1, w_all[0])
    spread_drain(2, w_next)
    spread_drain(3, w_all[1])
    for layer in range(LAYERS):
        wait_bytes(out_send.at[layer, pl.ds(0, HEADS - 1)], cross_ssem.at[layer])
    for n in range(1, LAYERS * NZ):
        wait_bytes(ybuf[n].at[pl.ds(0, 2 * (NY - 1))], y_ssem.at[n])
    wait_bytes(pack[0], z_ssem.at[0])
    wait_bytes(att_send[0].at[pl.ds(0, HEADS - 1)], att_ssem.at[0])
    z_wait(1)
    attend(1)
    out[...] = finish(1).astype(BF16)
    wait_bytes(pack[1], z_ssem.at[1])
    wait_bytes(att_send[1].at[pl.ds(0, HEADS - 1)], att_ssem.at[1])


def both(shape, dtype=BF16):
    return [pltpu.VMEM(shape, dtype)] * LAYERS


def ask(lengths, owners, pool):
    dma = pltpu.SemaphoreType.DMA
    vmem = pl.BlockSpec(memory_space=pltpu.VMEM)
    smem = pl.BlockSpec(memory_space=pltpu.SMEM)
    return pl.pallas_call(
        request_kernel,
        out_shape=(
            jax.ShapeDtypeStruct((1, 128), jnp.int32),
            jax.ShapeDtypeStruct((NZ, 1, 128), jnp.int32),
            jax.ShapeDtypeStruct((2 * NY, PAGE, 2 * DH), BF16),
            jax.ShapeDtypeStruct((1,), jnp.int32),
        ),
        in_specs=[smem, smem, pl.BlockSpec(memory_space=pl.ANY)],
        out_specs=(vmem, vmem, vmem, smem),
        scratch_shapes=[
            pltpu.VMEM((NZ, 1, 128), jnp.int32),
            pltpu.VMEM((1, 1, 128), jnp.int32),
            pltpu.VMEM((NY, 1, 128), jnp.int32),
            pltpu.VMEM((1, 128), jnp.int32),
            pltpu.SMEM((1, 128), jnp.int32),
            *[dma] * 7,
        ],
        compiler_params=pltpu.CompilerParams(collective_id=0, has_side_effects=True),
    )(lengths, owners, pool)


def run(turn, *args):
    C = CAPS[turn]
    dma = pltpu.SemaphoreType.DMA
    vmem = pl.BlockSpec(memory_space=pltpu.VMEM)
    smem = pl.BlockSpec(memory_space=pltpu.SMEM)
    return pl.pallas_call(
        functools.partial(kernel, C),
        out_shape=jax.ShapeDtypeStruct((BLOCK, D), BF16),
        in_specs=[
            smem,
            smem,
            smem,
            vmem,
            vmem,
            vmem,
            vmem,
            pl.BlockSpec(memory_space=pl.ANY),
        ],
        out_specs=vmem,
        scratch_shapes=[
            *both((NZ * C + 1, PAGE, 2 * DH)),
            *both((NZ - 1, C, PAGE, 2 * DH)),
            *both((HEADS, DH, D)),
            *both((HEADS, BLOCK, DH)),
            *both((HEADS, BLOCK, DH)),
            *both((HEADS, BLOCK, DH)),
            *both((HEADS, BLOCK, DH)),
            *[pltpu.VMEM((2 * NY, PAGE, 2 * DH), BF16)] * (LAYERS * NZ - 1),
            pltpu.VMEM((HEADS, BLOCK, D), BF16),
            pltpu.VMEM((HEADS, D, 4 * DH), BF16),
            pltpu.VMEM((HEADS, BLOCK, DH), BF16),
            pltpu.VMEM((HEADS, BLOCK, DH), BF16),
            pltpu.VMEM((HEADS, BLOCK, DH), F32),
            pltpu.VMEM((LAYERS, HEADS, BLOCK, DH), BF16),
            pltpu.VMEM((PAGES * PAGE, DH), BF16),
            pltpu.VMEM((PAGES * PAGE, DH), BF16),
            pltpu.VMEM((BLOCK, D), F32),
            dma((LAYERS * NZ,)),
            dma((LAYERS * NZ,)),
            dma((LAYERS,)),
            dma((LAYERS,)),
            dma((4,)),
            dma((4, HEADS)),
            dma((LAYERS,)),
            dma((LAYERS,)),
            dma((LAYERS,)),
            dma((LAYERS,)),
        ],
        compiler_params=pltpu.CompilerParams(
            collective_id=turn + 1, has_side_effects=True, vmem_limit_bytes=62 * 2**20
        ),
    )(*args)


def shards(candidates, proj_in, proj_out, page_pool, page_owner, history_pages):
    pool = page_pool[0]
    src, req, y_first, level = ask(history_pages, page_owner.transpose(0, 2, 1), pool)
    args = (history_pages, src, req, candidates, proj_in, proj_out, y_first, pool)
    return lax.switch(level[0], [functools.partial(run, turn, *args) for turn in range(len(CAPS))])


def solution(mesh):
    return jax.shard_map(
        shards,
        mesh=mesh,
        in_specs=(
            P(("cache", "head"), None),
            P(None, None, "head"),
            P(None, "head", None),
            P("cache", None, None, None, None, "head"),
            P("cache", None, None),
            P("cache"),
        ),
        out_specs=P(("cache", "head"), None),
        check_vma=False,
    )
```
